512 devices in a mesh: rep: 16 (over z), exp: 32 (over y, x, core).
Axes of the slice: x: 4, y: 4, z: 16, core: 2. Of those that a mesh axis runs over, the one named last changes fastest.
Arguments:
- tokens: bfloat16 [256, 512, 512], P('rep', 'exp'), may hold values from -48 to 48
- gate: float32 [256, 512], P('rep', 'exp'), may hold values from 0.25 to 1
- route: int32 [16, 32, 256, 1], P('rep', 'exp'), may hold values from 0 to 31; in each aligned block of 256 rows (0 to 255, 256 to 511, ..., all dimensions but the last counted through in order) at most 12 rows name the same one
- cotangent: bfloat16 [256, 512, 512], P('rep', 'exp'), may hold values from -6 to 6
- w_qkv: bfloat16 [512, 1536], replicated, may hold values from -1 to 1
- w_proj: bfloat16 [512, 512], replicated, may hold values from -0.25 to 0.25
- w_up: bfloat16 [32, 2048, 512], P('exp', 'rep'), may hold values from -0.25 to 0.25
- w_down: bfloat16 [32, 2048, 512], P('exp', 'rep'), may hold values from -0.125 to 0.125
Outputs:
- layer_out: bfloat16 [256, 512, 512], P('rep', 'exp')
- input_grad: bfloat16 [256, 512, 512], P('rep', 'exp')
- grad_up: float32 [32, 2048, 512], P('exp', 'rep')
- grad_down: float32 [32, 2048, 512], P('exp', 'rep')
The draws below stay inside these ranges and needn't reach their ends.
Inputs may be any that keep to these rules, and one draw needn't show every extreme that they name: `route`: among the tokens of one tile no expert is named more than 12 times.
All inputs are finite; a program needn't handle non-finite values.
Results may differ from the reference program's by a relative error of at most 0.018.
Values may be sent and summed in bfloat16 or wider, within the bound.
No kernel may reach another device: no remote copies, remote signals or barrier semaphores. Data moves between devices by JAX's collectives and lax.ppermute only.
A program may use at most 64 MiB of HBM per device.

```python
import math
import jax
import jax.numpy as jnp
import numpy as np
from jax import lax

D = 512
FF = 2048
HEADS = 16
TROWS = 16
TCOLS = 16
EXPERTS = 32
TOK_DEV = 256
CAP = 12
ROWS = 256
COLS = 512
N_REP = 16
N_EXP = 32


def draw_tokens(key, part):
    key_base = jax.random.fold_in(jax.random.fold_in(key, 11), 0)
    base = jax.random.normal(key_base, (ROWS, COLS, D), jnp.float32)
    return jnp.clip(base, -48.0, 48.0).astype(jnp.bfloat16)


def draw_w_qkv(key, part):
    key_main = jax.random.fold_in(jax.random.fold_in(key, 23), 0)
    matrix = jnp.clip(jax.random.normal(key_main, (D, 3 * D), jnp.float32), -6.0, 6.0) / jnp.sqrt(jnp.float32(D))
    return matrix.astype(jnp.bfloat16)


def steps_of(key, extent, cuts, smallest, high):
    loudness, own = 1.0, jax.random.fold_in(key, 6)
    for dim, shards_of in cuts:
        draws = jnp.exp(jax.random.uniform(jax.random.fold_in(own, dim), (shards_of,), jnp.float32, smallest / len(cuts), high / len(cuts)))
        loudness = loudness * jnp.repeat(draws, extent[dim] // shards_of).reshape([-1 if axis == dim else 1 for axis in range(len(extent))])
    return loudness


def assign_block(own_key, own, number, rows, amount, top, limit, slope):
    ranking = jax.random.permutation(own_key, amount)
    packed, common = shares(amount, rows * top, limit, slope, True), shares(amount, rows * top, limit, slope, False)
    places = jnp.arange(amount)

    def named(sizes, offset_by):
        used = int((sizes > 0).sum())
        fixed = max(1, used // 4)
        shifted = fixed + (places - fixed + offset_by * (used - fixed)) % max(1, amount - fixed)
        return jnp.zeros((amount,), jnp.int32).at[ranking[jnp.where(places < fixed, places, shifted)]].set(jnp.asarray(sizes, jnp.int32))

    sizes = jnp.where(number % 4 == 0, named(packed, number // 4), named(common, number - number // 4 - 1))
    mixed = jax.random.permutation(jax.random.fold_in(own, 3), amount)
    source_of, receiver = mixed[0:amount // 2 * 2:2], mixed[1:amount // 2 * 2:2]
    margin = jnp.minimum(sizes[source_of] - 1, limit - sizes[receiver]) // 2
    margin = jnp.where((source_of == ranking[0]) | (receiver == ranking[0]) | (sizes[receiver] == 0), 0, jnp.maximum(margin, 0))
    shifted = jax.random.randint(jax.random.fold_in(own, 4), (amount // 2,), 0, 1 << 20) % (margin + 1)
    sizes = sizes.at[source_of].add(-shifted).at[receiver].add(shifted)
    members = jnp.searchsorted(jnp.cumsum(sizes), jnp.arange(rows * top), side="right").astype(jnp.int32)
    listing = members.reshape(top, rows).T
    listing = listing[jax.random.permutation(jax.random.fold_in(own, 1), rows)]
    offset_by = jax.random.randint(jax.random.fold_in(own, 2), (rows, 1), 0, top)
    return jnp.take_along_axis(listing, (jnp.arange(top)[None, :] + offset_by) % top, axis=1)


def shares(amount, total, most, lean, full):
    loads = [(1 << 20) // math.isqrt(rank ** lean) + 1 for rank in range(1, amount + 1)]
    largest = most if full else min(most, max(-(-total // amount), total * loads[0] // sum(loads)))
    least = 1 if total - largest >= amount - 1 else 0
    holding, rest = [largest] + [least] * (amount - 1), total - largest - least * (amount - 1)
    while rest > 0:
        movable = [i for i in range(1, amount) if holding[i] < largest] or [i for i in range(1, amount) if holding[i] < most]
        pool, remaining = sum([loads[i] for i in movable]), rest
        for i in movable:
            addition = min(most - holding[i], max(1, remaining * loads[i] // pool), rest)
            holding[i] = holding[i] + addition
            rest = rest - addition
    return np.array(holding)


def normal_values(own_key, shape, width, most, cuts=(), kind=jnp.bfloat16):
    gain = steps_of(own_key, shape, cuts, -0.22, 0.18) if cuts else 1.0
    result = jax.random.normal(own_key, shape, jnp.float32) * width * gain
    return jnp.minimum(jnp.maximum(result, -most), most).astype(kind)


def setup_inputs(seed: int = 0) -> dict:
    splits = jax.random.split(jax.random.key(seed), 9)
    tokens = draw_tokens(jax.random.fold_in(splits[8], 71), 0)
    gate = jnp.clip(0.25 + 0.75 * jax.random.uniform(splits[1], (ROWS, COLS), jnp.float32) ** steps_of(splits[1], (ROWS, COLS), ((0, 16), (1, 32)), -0.2, 0.2), 0.25, 1.0)
    route_keys = jax.random.split(jax.random.fold_in(splits[2], 1), N_REP * N_EXP * TOK_DEV // TOK_DEV)
    route_turns = jax.random.permutation(jax.random.fold_in(splits[2], 3), N_REP * N_EXP * TOK_DEV // TOK_DEV)
    route = jax.vmap(lambda own, number: assign_block(jax.random.fold_in(splits[2], 2), own, number, TOK_DEV, EXPERTS, 1, CAP, 2))(route_keys, route_turns).reshape((N_REP, N_EXP, TOK_DEV, 1))
    cotangent = normal_values(splits[3], (ROWS, COLS, D), 1.0, 6.0, ((0, 16), (1, 32)))
    w_qkv = draw_w_qkv(jax.random.fold_in(splits[8], 71), 0)
    w_proj = normal_values(splits[5], (D, D), D ** -0.5, 0.25)
    w_up = normal_values(splits[6], (EXPERTS, FF, D), D ** -0.5, 0.25, ((0, 32), (1, 16)))
    w_down = normal_values(splits[7], (EXPERTS, FF, D), FF ** -0.5, 0.125, ((0, 32), (1, 16)))
    return {"tokens": tokens, "gate": gate, "route": route, "cotangent": cotangent, "w_qkv": w_qkv, "w_proj": w_proj, "w_up": w_up, "w_down": w_down}


GELU_C = math.sqrt(2.0 / math.pi)
window_side = 8
margin_cells = 4

def gelu_tanh(inputs):
    return 0.5 * inputs * (1.0 + jnp.tanh(GELU_C * (inputs + 0.044715 * inputs * inputs * inputs)))

def gelu_slope(inputs):
    inner = jnp.tanh(GELU_C * (inputs + 0.044715 * inputs * inputs * inputs))
    return 0.5 * (1.0 + inner) + 0.5 * inputs * (1.0 - inner * inner) * GELU_C * (1.0 + 3.0 * 0.044715 * inputs * inputs)

def layer_norm(values):
    average = lax.optimization_barrier(jnp.mean(values, axis=-1, keepdims=True))
    centred = values - average
    spread = lax.optimization_barrier(jnp.mean(centred * centred, axis=-1, keepdims=True))
    return centred * lax.rsqrt(spread + 1e-05)

def window_attend(qkv, in_grid):
    ext_rows, ext_cols, triple = qkv.shape
    feature = triple // 3
    head_size = feature // HEADS
    win_rows = ext_rows // window_side
    win_cols = ext_cols // window_side
    cells = window_side * window_side
    blocks = qkv.reshape(win_rows, window_side, win_cols, window_side, triple).transpose(0, 2, 1, 3, 4)
    blocks = blocks.reshape(win_rows * win_cols, cells, 3, HEADS, head_size)
    present = in_grid.reshape(win_rows, window_side, win_cols, window_side).transpose(0, 2, 1, 3).reshape(win_rows * win_cols, cells)
    queries = blocks[:, :, 0].astype(jnp.float32)
    key_part = blocks[:, :, 1].astype(jnp.float32)
    value_part = blocks[:, :, 2].astype(jnp.float32)
    scores = jnp.einsum('wqhd,wkhd->whqk', queries, key_part) / math.sqrt(head_size)
    scores = jnp.where(present[:, None, None, :], scores, jnp.float32(-1e+30))
    peak_score = lax.optimization_barrier(jnp.max(scores, axis=-1, keepdims=True))
    weights = jnp.exp(scores - peak_score)
    probabilities = (weights / lax.optimization_barrier(jnp.sum(weights, axis=-1, keepdims=True))).astype(jnp.bfloat16)
    context = jnp.einsum('whqk,wkhd->wqhd', probabilities.astype(jnp.float32), value_part).astype(jnp.bfloat16)
    context = context.reshape(win_rows, win_cols, window_side, window_side, feature).transpose(0, 2, 1, 3, 4)
    return context.reshape(ext_rows, ext_cols, feature)

def to_devices(values):
    return values.reshape(N_REP, TROWS, N_EXP, TCOLS, -1).transpose(0, 2, 1, 3, 4).reshape(N_REP, N_EXP, TOK_DEV, -1)

def to_grid(values):
    return values.reshape(N_REP, N_EXP, TROWS, TCOLS, -1).transpose(0, 2, 1, 3, 4).reshape(N_REP * TROWS, N_EXP * TCOLS, -1)

def one_replica(slot_rows, slot_grads, up_mat, down_mat):
    pre_act = jnp.dot(slot_rows, up_mat.T, preferred_element_type=jnp.float32)
    hidden = gelu_tanh(pre_act).astype(jnp.bfloat16)
    expert_out = jnp.dot(hidden, down_mat, preferred_element_type=jnp.float32).astype(jnp.bfloat16)
    hidden_grad = jnp.dot(slot_grads, down_mat.T, preferred_element_type=jnp.float32)
    pre_grad = (hidden_grad * gelu_slope(pre_act)).astype(jnp.bfloat16)
    input_slots = jnp.dot(pre_grad, up_mat, preferred_element_type=jnp.float32).astype(jnp.bfloat16)
    part_up = jnp.dot(pre_grad.T, slot_rows, preferred_element_type=jnp.float32).astype(jnp.bfloat16)
    part_down = jnp.dot(hidden.T, slot_grads, preferred_element_type=jnp.float32).astype(jnp.bfloat16)
    return (expert_out, input_slots, part_up, part_down)

def one_expert(operands):
    rows_all, grads_all, up_mat, down_mat = operands
    expert_out, input_slots, part_up, part_down = jax.vmap(one_replica, in_axes=(0, 0, None, None))(rows_all, grads_all, up_mat, down_mat)
    grad_up = lax.optimization_barrier(jnp.sum(part_up.astype(jnp.float32), axis=0)) / N_REP
    grad_down = lax.optimization_barrier(jnp.sum(part_down.astype(jnp.float32), axis=0)) / N_REP
    return (expert_out, input_slots, grad_up, grad_down)

def reference(tokens, gate, route, cotangent, w_qkv, w_proj, w_up, w_down):
    grid_rows, grid_cols, feature = tokens.shape
    padded = jnp.pad(tokens, ((margin_cells, margin_cells), (margin_cells, margin_cells), (0, 0)))
    ext_rows = grid_rows + 2 * margin_cells
    ext_cols = grid_cols + 2 * margin_cells
    qkv_all = jnp.dot(padded.reshape(-1, feature), w_qkv, preferred_element_type=jnp.float32).astype(jnp.bfloat16)
    qkv_all = qkv_all.reshape(ext_rows, ext_cols, 3 * feature)
    row_ids = jnp.arange(ext_rows, dtype=jnp.int32) - margin_cells
    col_ids = jnp.arange(ext_cols, dtype=jnp.int32) - margin_cells
    in_grid = ((row_ids >= 0) & (row_ids < grid_rows))[:, None] & ((col_ids >= 0) & (col_ids < grid_cols))[None, :]
    context = window_attend(qkv_all, in_grid)[margin_cells:grid_rows + margin_cells, margin_cells:grid_cols + margin_cells].reshape(-1, feature)
    attended = jnp.dot(context, w_proj, preferred_element_type=jnp.float32)
    mixed = (tokens.reshape(-1, feature).astype(jnp.float32) + layer_norm(attended)).astype(jnp.bfloat16)
    mixed_dev = to_devices(mixed.reshape(grid_rows, grid_cols, feature))
    gate_dev = to_devices(gate[:, :, None])[..., 0]
    upstream = (gate[:, :, None] * cotangent.astype(jnp.float32)).astype(jnp.bfloat16)
    upstream_dev = to_devices(upstream)
    chosen = route[..., 0]
    matches = (chosen[..., None] == jnp.arange(EXPERTS, dtype=jnp.int32)).astype(jnp.int32)
    position = lax.optimization_barrier(jnp.sum(matches * (jnp.cumsum(matches, axis=2) - 1), axis=-1)).astype(jnp.int32)
    replica = jnp.arange(N_REP, dtype=jnp.int32)[:, None, None]
    source = jnp.arange(N_EXP, dtype=jnp.int32)[None, :, None]
    target = (((replica * EXPERTS + chosen) * N_EXP + source) * CAP + position).reshape(-1).astype(jnp.int32)
    total = N_REP * EXPERTS * N_EXP * CAP
    slots_x = jnp.zeros((total, feature), jnp.bfloat16).at[target].set(mixed_dev.reshape(-1, feature))
    slots_g = jnp.zeros((total, feature), jnp.bfloat16).at[target].set(upstream_dev.reshape(-1, feature))
    slots_x = slots_x.reshape(N_REP, EXPERTS, N_EXP * CAP, feature).transpose(1, 0, 2, 3)
    slots_g = slots_g.reshape(N_REP, EXPERTS, N_EXP * CAP, feature).transpose(1, 0, 2, 3)
    expert_out, input_slots, grad_up, grad_down = lax.map(one_expert, (slots_x, slots_g, w_up, w_down))
    out_flat = expert_out.transpose(1, 0, 2, 3).reshape(total, feature)
    back_flat = input_slots.transpose(1, 0, 2, 3).reshape(total, feature)
    out_tok = out_flat[target].reshape(N_REP, N_EXP, TOK_DEV, feature).astype(jnp.float32)
    grad_tok = back_flat[target].reshape(N_REP, N_EXP, TOK_DEV, feature)
    layer_dev = (mixed_dev.astype(jnp.float32) + gate_dev[..., None] * out_tok).astype(jnp.bfloat16)
    return (to_grid(layer_dev), to_grid(grad_tok), grad_up, grad_down)
```

```python
import math

import jax
import jax.numpy as jnp
from jax import lax
from jax.experimental import pallas as pl
from jax.experimental.pallas import tpu as pltpu
from jax.sharding import PartitionSpec as P

HEADS = 16


GELU_C = math.sqrt(2.0 / math.pi)
window_side = 8
margin_cells = 4
CHUNKS = 8

VMEM_LIMIT = 48 * 1024 * 1024


def padded(block, sides, width):
    for axis, dim in sides:
        count = lax.axis_size(axis)
        forward = [(i, i + 1) for i in range(count - 1)]
        backward = [(target, source) for source, target in forward]
        low = lax.ppermute(
            lax.slice_in_dim(block, block.shape[dim] - width, None, axis=dim), axis, forward
        )
        high = lax.ppermute(lax.slice_in_dim(block, 0, width, axis=dim), axis, backward)
        block = jnp.concatenate([low, block, high], axis=dim)
    return block


def in_one_piece(arrays, axis, split_dim, concat_dim, along):
    both = jnp.concatenate(arrays, axis=along)
    result, at, finished = (
        lax.all_to_all(both, axis, split_axis=split_dim, concat_axis=concat_dim, tiled=True),
        0,
        [],
    )
    for a in arrays:
        finished.append(lax.slice_in_dim(result, at, at + a.shape[along], axis=along))
        at += a.shape[along]
    return tuple(finished)


def layer_norm(values):
    average = jnp.mean(values, axis=-1, keepdims=True)
    centred = values - average
    spread = jnp.mean(centred * centred, axis=-1, keepdims=True)
    return centred * lax.rsqrt(spread + 1e-05)


def window_attend(qkv, in_grid):
    ext_rows, ext_cols, triple = qkv.shape
    feature = triple // 3
    head_size = feature // HEADS
    win_rows = ext_rows // window_side
    win_cols = ext_cols // window_side
    cells = window_side * window_side
    blocks = qkv.reshape(win_rows, window_side, win_cols, window_side, triple).transpose(
        0, 2, 1, 3, 4
    )
    blocks = blocks.reshape(win_rows * win_cols, cells, 3, HEADS, head_size)
    present = (
        in_grid.reshape(win_rows, window_side, win_cols, window_side)
        .transpose(0, 2, 1, 3)
        .reshape(win_rows * win_cols, cells)
    )
    scores = jnp.einsum(
        "wqhd,wkhd->whqk", blocks[:, :, 0], blocks[:, :, 1], preferred_element_type=jnp.float32
    ) / math.sqrt(head_size)
    scores = jnp.where(present[:, None, None, :], scores, jnp.float32(-1e30))
    peak_score = jnp.max(scores, axis=-1, keepdims=True)
    weights = jnp.exp(scores - peak_score)
    probabilities = (weights / jnp.sum(weights, axis=-1, keepdims=True)).astype(jnp.bfloat16)
    context = jnp.einsum(
        "whqk,wkhd->wqhd", probabilities, blocks[:, :, 2], preferred_element_type=jnp.float32
    ).astype(jnp.bfloat16)
    context = context.reshape(win_rows, win_cols, window_side, window_side, feature).transpose(
        0, 2, 1, 3, 4
    )
    return context.reshape(ext_rows, ext_cols, feature)


def nt(a, b):
    return lax.dot_general(a, b, (((1,), (1,)), ((), ())), preferred_element_type=jnp.float32)


def tn(a, b):
    return lax.dot_general(a, b, (((0,), (0,)), ((), ())), preferred_element_type=jnp.float32)


def middle_kernel(w_ref, x_ref, g_ref, grads_ref, hid_ref, pg_ref):
    shards, _, width, feature = w_ref.shape
    up = w_ref[:, 0].reshape(shards * width, feature)
    down = w_ref[:, 1].reshape(shards * width, feature)
    x, g = x_ref[...], g_ref[...]
    pre = nt(up, x)
    square = pre * pre
    inner = jnp.tanh(pre * (GELU_C + (GELU_C * 0.044715) * square))
    half = 0.5 + 0.5 * inner
    hidden = (pre * half).astype(jnp.bfloat16)
    slope = half + (0.5 * pre) * (1.0 - inner * inner) * (
        GELU_C + (3.0 * 0.044715 * GELU_C) * square
    )
    pre_grad = (nt(down, g) * slope).astype(jnp.bfloat16)
    hid_ref[...] = hidden
    pg_ref[...] = pre_grad
    grad_up = jnp.dot(pre_grad, x, preferred_element_type=jnp.float32).astype(jnp.bfloat16)
    grad_down = jnp.dot(hidden, g, preferred_element_type=jnp.float32).astype(jnp.bfloat16)
    grads_ref[:, :width] = grad_up.reshape(shards, width, feature)
    grads_ref[:, width:] = grad_down.reshape(shards, width, feature)


def middle(weights, slot_x, slot_g):
    owners, _, width, feature = weights.shape
    rows = slot_x.shape[0]
    step = owners // CHUNKS
    ff = owners * width
    return pl.pallas_call(
        middle_kernel,
        grid=(CHUNKS,),
        in_specs=[
            pl.BlockSpec((step, 2, width, feature), lambda i: (i, 0, 0, 0)),
            pl.BlockSpec((rows, feature), lambda i: (0, 0)),
            pl.BlockSpec((rows, feature), lambda i: (0, 0)),
        ],
        out_specs=[
            pl.BlockSpec((step, 2 * width, feature), lambda i: (i, 0, 0)),
            pl.BlockSpec((step * width, rows), lambda i: (i, 0)),
            pl.BlockSpec((step * width, rows), lambda i: (i, 0)),
        ],
        out_shape=[
            jax.ShapeDtypeStruct((owners, 2 * width, feature), jnp.bfloat16),
            jax.ShapeDtypeStruct((ff, rows), jnp.bfloat16),
            jax.ShapeDtypeStruct((ff, rows), jnp.bfloat16),
        ],
        compiler_params=pltpu.CompilerParams(vmem_limit_bytes=VMEM_LIMIT),
        cost_estimate=pl.CostEstimate(
            flops=8 * rows * ff * feature,
            bytes_accessed=8 * ff * feature + 4 * ff * rows,
            transcendentals=ff * rows,
        ),
        name="middle",
    )(weights, slot_x, slot_g)


def back_kernel(w_ref, hid_ref, pg_ref, out_ref, in_ref, out_acc, in_acc):
    shards, _, width, feature = w_ref.shape
    up = w_ref[:, 0].reshape(shards * width, feature)
    down = w_ref[:, 1].reshape(shards * width, feature)

    @pl.when(pl.program_id(0) == 0)
    def _():
        out_acc[...] = jnp.zeros_like(out_acc)
        in_acc[...] = jnp.zeros_like(in_acc)

    out_acc[...] += tn(hid_ref[...], down)
    in_acc[...] += tn(pg_ref[...], up)

    @pl.when(pl.program_id(0) == pl.num_programs(0) - 1)
    def _():
        out_ref[...] = out_acc[...].astype(jnp.bfloat16)
        in_ref[...] = in_acc[...].astype(jnp.bfloat16)


def back(weights, hidden, pre_grad):
    owners, _, width, feature = weights.shape
    ff, rows = hidden.shape
    steps = 4
    step = owners // steps
    return pl.pallas_call(
        back_kernel,
        grid=(steps,),
        in_specs=[
            pl.BlockSpec((step, 2, width, feature), lambda i: (i, 0, 0, 0)),
            pl.BlockSpec((step * width, rows), lambda i: (i, 0)),
            pl.BlockSpec((step * width, rows), lambda i: (i, 0)),
        ],
        out_specs=[
            pl.BlockSpec((rows, feature), lambda i: (0, 0)),
            pl.BlockSpec((rows, feature), lambda i: (0, 0)),
        ],
        out_shape=[jax.ShapeDtypeStruct((rows, feature), jnp.bfloat16)] * 2,
        scratch_shapes=[pltpu.VMEM((rows, feature), jnp.float32)] * 2,
        compiler_params=pltpu.CompilerParams(vmem_limit_bytes=VMEM_LIMIT),
        cost_estimate=pl.CostEstimate(
            flops=4 * rows * ff * feature,
            bytes_accessed=4 * ff * feature + 4 * ff * rows,
            transcendentals=0,
        ),
        name="back",
    )(weights, hidden, pre_grad)


def per_device(tokens, gate, route, cotangent, w_qkv, w_proj, w_up, w_down):
    tile_rows, tile_cols, feature = tokens.shape
    tok_count = tile_rows * tile_cols
    ext_rows = tile_rows + 2 * margin_cells
    ext_cols = tile_cols + 2 * margin_cells
    weights = lax.all_gather(
        jnp.concatenate([w_up, w_down], axis=0), "rep", axis=0, tiled=False
    )
    extended = padded(tokens, (("rep", 0), ("exp", 1)), 4)
    qkv = jnp.dot(extended.reshape(-1, feature), w_qkv, preferred_element_type=jnp.float32).astype(
        jnp.bfloat16
    )
    qkv = qkv.reshape(ext_rows, ext_cols, 3 * feature)
    row_ids = (
        lax.axis_index("rep") * tile_rows - margin_cells + jnp.arange(ext_rows, dtype=jnp.int32)
    )
    col_ids = (
        lax.axis_index("exp") * tile_cols - margin_cells + jnp.arange(ext_cols, dtype=jnp.int32)
    )
    row_inside = (row_ids >= 0) & (row_ids < tile_rows * lax.axis_size("rep"))
    col_inside = (col_ids >= 0) & (col_ids < tile_cols * lax.axis_size("exp"))
    in_grid = row_inside[:, None] & col_inside[None, :]
    context = window_attend(qkv, in_grid)[
        margin_cells : tile_rows + margin_cells, margin_cells : tile_cols + margin_cells
    ].reshape(tok_count, feature)
    attended = jnp.dot(context, w_proj, preferred_element_type=jnp.float32)
    flat_tokens = tokens.reshape(tok_count, feature)
    mixed = (flat_tokens.astype(jnp.float32) + layer_norm(attended)).astype(jnp.bfloat16)
    experts = lax.axis_size("exp")
    capacity = max(2, 3 * tok_count // (2 * experts))
    chosen = route.reshape(tok_count)
    matches = chosen[:, None] == jnp.arange(experts, dtype=jnp.int32)[None, :]
    earlier = jnp.arange(tok_count)[:, None] > jnp.arange(tok_count)[None, :]
    before = jnp.dot(
        earlier.astype(jnp.bfloat16),
        matches.astype(jnp.bfloat16),
        preferred_element_type=jnp.float32,
    )
    position = jnp.sum(jnp.where(matches, before, 0.0), axis=1).astype(jnp.int32)
    target = chosen * capacity + position
    placer = (target[:, None] == jnp.arange(experts * capacity, dtype=jnp.int32)[None, :]).astype(
        jnp.bfloat16
    )
    gate_rows = gate.reshape(tok_count)
    upstream = (
        gate_rows[:, None] * cotangent.reshape(tok_count, feature).astype(jnp.float32)
    ).astype(jnp.bfloat16)

    def to_slots(values):
        placed = lax.dot_general(
            placer, values, (((0,), (0,)), ((), ())), preferred_element_type=jnp.float32
        )
        return placed.astype(jnp.bfloat16).reshape(experts, capacity, feature)

    def from_slots(slot_values):
        return jnp.dot(
            placer,
            slot_values.reshape(experts * capacity, feature),
            preferred_element_type=jnp.float32,
        )

    sent_x, sent_g = in_one_piece((to_slots(mixed), to_slots(upstream)), "exp", 0, 0, 1)
    slot_rows = sent_x.reshape(-1, feature)
    slot_grads = sent_g.reshape(-1, feature)
    grads, hidden, pre_grad = middle(weights, slot_rows, slot_grads)
    summed = lax.psum_scatter(grads, "rep", scatter_dimension=0, tiled=True)[0]
    expert_out, input_slots = back(weights, hidden, pre_grad)
    back_out, back_grad = in_one_piece(
        (
            expert_out.reshape(-1, capacity, feature),
            input_slots.reshape(-1, capacity, feature),
        ),
        "exp",
        0,
        0,
        1,
    )
    layer_out = (mixed.astype(jnp.float32) + gate_rows[:, None] * from_slots(back_out)).astype(
        jnp.bfloat16
    )
    input_grad = from_slots(back_grad).astype(jnp.bfloat16)
    average_factor = 1.0 / lax.axis_size("rep")
    width = w_up.shape[1]
    total = summed.astype(jnp.float32) * average_factor
    return (
        layer_out.reshape(tile_rows, tile_cols, feature),
        input_grad.reshape(tile_rows, tile_cols, feature),
        total[:width][None],
        total[width:][None],
    )


def solution(mesh):
    placed = (
        P("rep", "exp", None),
        P("rep", "exp"),
        P("rep", "exp", None, None),
        P("rep", "exp", None),
        P(),
        P(),
        P("exp", "rep", None),
        P("exp", "rep", None),
    )
    return jax.shard_map(
        per_device,
        mesh=mesh,
        in_specs=placed,
        out_specs=(
            P("rep", "exp", None),
            P("rep", "exp", None),
            P("exp", "rep", None),
            P("exp", "rep", None),
        ),
        check_vma=False,
    )
```

```python
import functools
import math

import jax
import jax.numpy as jnp
import numpy as np
from jax import lax
from jax.experimental import pallas as pl
from jax.experimental.pallas import tpu as pltpu
from jax.sharding import PartitionSpec as P

HEADS = 16


GELU_C = math.sqrt(2.0 / math.pi)
window_side = 8
margin_cells = 4
CHUNKS = 8

VMEM_LIMIT = 48 * 1024 * 1024


def nt(a, b):
    return lax.dot_general(a, b, (((1,), (1,)), ((), ())), preferred_element_type=jnp.float32)


def tn(a, b):
    return lax.dot_general(a, b, (((0,), (0,)), ((), ())), preferred_element_type=jnp.float32)


def middle_kernel(w_ref, x_ref, g_ref, grads_ref, hid_ref, pg_ref):
    shards, _, width, feature = w_ref.shape
    up = w_ref[:, 0].reshape(shards * width, feature)
    down = w_ref[:, 1].reshape(shards * width, feature)
    x, g = x_ref[...], g_ref[...]
    pre = nt(up, x)
    square = pre * pre
    inner = jnp.tanh(pre * (GELU_C + (GELU_C * 0.044715) * square))
    half = 0.5 + 0.5 * inner
    hidden = (pre * half).astype(jnp.bfloat16)
    slope = half + (0.5 * pre) * (1.0 - inner * inner) * (
        GELU_C + (3.0 * 0.044715 * GELU_C) * square
    )
    pre_grad = (nt(down, g) * slope).astype(jnp.bfloat16)
    hid_ref[...] = hidden
    pg_ref[...] = pre_grad
    grad_up = jnp.dot(pre_grad, x, preferred_element_type=jnp.float32).astype(jnp.bfloat16)
    grad_down = jnp.dot(hidden, g, preferred_element_type=jnp.float32).astype(jnp.bfloat16)
    grads_ref[:, :width] = grad_up.reshape(shards, width, feature)
    grads_ref[:, width:] = grad_down.reshape(shards, width, feature)


def middle(weights, slot_x, slot_g):
    owners, _, width, feature = weights.shape
    rows = slot_x.shape[0]
    step = owners // CHUNKS
    ff = owners * width
    return pl.pallas_call(
        middle_kernel,
        grid=(CHUNKS,),
        in_specs=[
            pl.BlockSpec((step, 2, width, feature), lambda i: (i, 0, 0, 0)),
            pl.BlockSpec((rows, feature), lambda i: (0, 0)),
            pl.BlockSpec((rows, feature), lambda i: (0, 0)),
        ],
        out_specs=[
            pl.BlockSpec((step, 2 * width, feature), lambda i: (i, 0, 0)),
            pl.BlockSpec((step * width, rows), lambda i: (i, 0)),
            pl.BlockSpec((step * width, rows), lambda i: (i, 0)),
        ],
        out_shape=[
            jax.ShapeDtypeStruct((owners, 2 * width, feature), jnp.bfloat16),
            jax.ShapeDtypeStruct((ff, rows), jnp.bfloat16),
            jax.ShapeDtypeStruct((ff, rows), jnp.bfloat16),
        ],
        compiler_params=pltpu.CompilerParams(vmem_limit_bytes=VMEM_LIMIT),
        cost_estimate=pl.CostEstimate(
            flops=8 * rows * ff * feature,
            bytes_accessed=8 * ff * feature + 4 * ff * rows,
            transcendentals=ff * rows,
        ),
        name="middle",
    )(weights, slot_x, slot_g)


def back_kernel(w_ref, hid_ref, pg_ref, out_ref, in_ref, out_acc, in_acc):
    shards, _, width, feature = w_ref.shape
    up = w_ref[:, 0].reshape(shards * width, feature)
    down = w_ref[:, 1].reshape(shards * width, feature)

    @pl.when(pl.program_id(0) == 0)
    def _():
        out_acc[...] = jnp.zeros_like(out_acc)
        in_acc[...] = jnp.zeros_like(in_acc)

    out_acc[...] += tn(hid_ref[...], down)
    in_acc[...] += tn(pg_ref[...], up)

    @pl.when(pl.program_id(0) == pl.num_programs(0) - 1)
    def _():
        out_ref[...] = out_acc[...].astype(jnp.bfloat16)
        in_ref[...] = in_acc[...].astype(jnp.bfloat16)


def back(weights, hidden, pre_grad):
    owners, _, width, feature = weights.shape
    ff, rows = hidden.shape
    steps = 4
    step = owners // steps
    return pl.pallas_call(
        back_kernel,
        grid=(steps,),
        in_specs=[
            pl.BlockSpec((step, 2, width, feature), lambda i: (i, 0, 0, 0)),
            pl.BlockSpec((step * width, rows), lambda i: (i, 0)),
            pl.BlockSpec((step * width, rows), lambda i: (i, 0)),
        ],
        out_specs=[
            pl.BlockSpec((rows, feature), lambda i: (0, 0)),
            pl.BlockSpec((rows, feature), lambda i: (0, 0)),
        ],
        out_shape=[jax.ShapeDtypeStruct((rows, feature), jnp.bfloat16)] * 2,
        scratch_shapes=[pltpu.VMEM((rows, feature), jnp.float32)] * 2,
        compiler_params=pltpu.CompilerParams(vmem_limit_bytes=VMEM_LIMIT),
        cost_estimate=pl.CostEstimate(
            flops=4 * rows * ff * feature,
            bytes_accessed=4 * ff * feature + 4 * ff * rows,
            transcendentals=0,
        ),
        name="back",
    )(weights, hidden, pre_grad)


def window_rows(side, margin, tile):
    ext = tile + 2 * margin
    wins = ext // side
    edge, strip = margin * tile, ext * margin
    into = np.zeros((ext * ext, ext * ext), np.float32)
    outof = np.zeros((tile * tile, ext * ext), np.float32)
    for r in range(ext):
        for c in range(ext):
            at = ((r // side) * wins + c // side) * side * side + (r % side) * side + c % side
            base = tile * tile
            if c < margin:
                piece = base + 2 * edge + r * margin + c
            elif c >= tile + margin:
                piece = base + 2 * edge + strip + r * margin + c - tile - margin
            elif r < margin:
                piece = base + r * tile + c - margin
            elif r >= tile + margin:
                piece = base + edge + (r - tile - margin) * tile + c - margin
            else:
                piece = (r - margin) * tile + c - margin
                outof[piece, at] = 1.0
            into[at, piece] = 1.0
    return into.astype(jnp.bfloat16), outof.astype(jnp.bfloat16)


def placers(target, slots, capacity):
    rows = lax.broadcasted_iota(jnp.int32, (2 * slots, target.shape[1]), 0)
    return rows == target, rows == target + capacity


def front_kernel(
    experts, capacity, at_ref, tok_ref, low_ref, high_ref, left_ref, right_ref, into_ref, outof_ref,
    wqkv_ref, wproj_ref, route_ref, gate_ref, cot_ref, mixed_ref, slots_ref, target_ref, qkv_ref, ctx_ref,
):
    bf16, f32 = jnp.bfloat16, jnp.float32
    tokens = tok_ref[...]
    count, feature = tokens.shape
    cells = window_side * window_side
    head = feature // HEADS
    group = 128 // head
    pieces = jnp.concatenate(
        [tokens, low_ref[...], high_ref[...], left_ref[...], right_ref[...]], axis=0
    )
    placed = jnp.dot(into_ref[...], pieces, preferred_element_type=f32).astype(bf16)
    qkv_ref[...] = jnp.dot(placed, wqkv_ref[...], preferred_element_type=f32).astype(bf16)
    first_row, last_row = at_ref[0] == 0, at_ref[0] == at_ref[1] - 1
    first_col, last_col = at_ref[2] == 0, at_ref[2] == at_ref[3] - 1
    lane = lax.broadcasted_iota(jnp.int32, (1, 128), 1)
    own = [
        ((lane >= h * head) & (lane < (h + 1) * head)).astype(f32) for h in range(group)
    ]
    own16 = [o.astype(bf16) for o in own]
    key = lax.broadcasted_iota(jnp.int32, (cells, 128), 0)
    key_row, key_col = key // window_side, key % window_side
    half = window_side // 2
    low_bias = jnp.float32(-1e30)
    edge_bias = {
        (0, 0): jnp.where(key_row < half, jnp.where(first_row, low_bias, 0.0), 0.0),
        (0, 2): jnp.where(key_row >= half, jnp.where(last_row, low_bias, 0.0), 0.0),
        (1, 0): jnp.where(key_col < half, jnp.where(first_col, low_bias, 0.0), 0.0),
        (1, 2): jnp.where(key_col >= half, jnp.where(last_col, low_bias, 0.0), 0.0),
    }
    scale = 1.0 / math.sqrt(head)
    for window in range(9):
        wi, wj = window // 3, window % 3
        bias = None
        if wi != 1:
            bias = edge_bias[0, wi]
        if wj != 1:
            bias = edge_bias[1, wj] if bias is None else bias + edge_bias[1, wj]
        if bias is not None:
            bias = jnp.concatenate([bias] * (group * cells // 128), axis=1)
        rows = slice(window * cells, (window + 1) * cells)
        for g in range(feature // 128):
            q = qkv_ref[rows, g * 128 : (g + 1) * 128]
            k = qkv_ref[rows, feature + g * 128 : feature + (g + 1) * 128]
            v = qkv_ref[rows, 2 * feature + g * 128 : 2 * feature + (g + 1) * 128]
            spread = jnp.concatenate([q * o for o in own16], axis=0)
            scores = nt(k, spread)
            if bias is not None:
                scores = scores + bias
            peak = jnp.max(scores, axis=0, keepdims=True)
            weights = jnp.exp((scores - peak) * scale)
            probs = (weights * (1.0 / jnp.sum(weights, axis=0, keepdims=True))).astype(bf16)
            wide = tn(probs, v)
            mine = wide[:cells] * own[0]
            for h in range(1, group):
                mine = mine + wide[h * cells : (h + 1) * cells] * own[h]
            ctx_ref[rows, g * 128 : (g + 1) * 128] = mine.astype(bf16)
    context = jnp.dot(outof_ref[...], ctx_ref[...], preferred_element_type=f32).astype(bf16)
    attended = jnp.dot(context, wproj_ref[...], preferred_element_type=f32)
    centred = attended - jnp.mean(attended, axis=-1, keepdims=True)
    spread_of = jnp.mean(centred * centred, axis=-1, keepdims=True)
    mixed = (tokens.astype(f32) + centred * lax.rsqrt(spread_of + 1e-05)).astype(bf16)
    mixed_ref[...] = mixed
    route = route_ref[...]
    matches = lax.broadcasted_iota(jnp.int32, (experts, count), 0) == route
    matches = matches.astype(f32)
    earlier = lax.broadcasted_iota(jnp.int32, (count, count), 0) < lax.broadcasted_iota(
        jnp.int32, (count, count), 1
    )
    before = jnp.dot(
        matches.astype(bf16), earlier.astype(f32).astype(bf16), preferred_element_type=f32
    )
    position = jnp.sum(matches * before, axis=0, keepdims=True).astype(jnp.int32)
    target = route * (2 * capacity) + position
    target_ref[...] = target
    upstream = (gate_ref[...] * cot_ref[...].astype(f32)).astype(bf16)
    place_x, place_g = placers(target, experts * capacity, capacity)
    slots = jnp.dot(place_x.astype(f32).astype(bf16), mixed, preferred_element_type=f32)
    slots = slots + jnp.dot(
        place_g.astype(f32).astype(bf16), upstream, preferred_element_type=f32
    )
    slots_ref[...] = slots.astype(bf16)


def front(at, tokens, low, high, left, right, w_qkv, w_proj, route, gate, cotangent, experts, capacity):
    count, feature = tokens.shape
    into, outof = window_rows(window_side, margin_cells, math.isqrt(count))
    ext = into.shape[0]
    vmem = pl.BlockSpec(memory_space=pltpu.VMEM)
    return pl.pallas_call(
        functools.partial(front_kernel, experts, capacity),
        in_specs=[pl.BlockSpec(memory_space=pltpu.SMEM)] + [vmem] * 12,
        out_specs=[vmem] * 3,
        out_shape=[
            jax.ShapeDtypeStruct((count, feature), jnp.bfloat16),
            jax.ShapeDtypeStruct((2 * experts * capacity, feature), jnp.bfloat16),
            jax.ShapeDtypeStruct((1, count), jnp.int32),
        ],
        scratch_shapes=[
            pltpu.VMEM((ext, 3 * feature), jnp.bfloat16),
            pltpu.VMEM((ext, feature), jnp.bfloat16),
        ],
        compiler_params=pltpu.CompilerParams(vmem_limit_bytes=VMEM_LIMIT),
        cost_estimate=pl.CostEstimate(
            flops=5_000_000_000, bytes_accessed=8_000_000, transcendentals=600_000
        ),
        name="front",
    )(
        at, tokens, low, high, left, right, jnp.asarray(into), jnp.asarray(outof),
        w_qkv, w_proj, route, gate, cotangent,
    )


def combine_kernel(capacity, back_ref, target_ref, mixed_ref, gate_ref, out_ref, grad_ref):
    f32 = jnp.float32
    back_rows = back_ref[...]
    place_x, place_g = placers(target_ref[...], back_rows.shape[0] // 2, capacity)
    token_out = tn(place_x.astype(f32).astype(jnp.bfloat16), back_rows)
    out_ref[...] = (mixed_ref[...].astype(f32) + gate_ref[...] * token_out).astype(jnp.bfloat16)
    grad_ref[...] = tn(place_g.astype(f32).astype(jnp.bfloat16), back_rows).astype(jnp.bfloat16)


def combine(returned, target, mixed, gate, capacity):
    vmem = pl.BlockSpec(memory_space=pltpu.VMEM)
    return pl.pallas_call(
        functools.partial(combine_kernel, capacity),
        in_specs=[vmem] * 4,
        out_specs=[vmem] * 2,
        out_shape=[jax.ShapeDtypeStruct(mixed.shape, jnp.bfloat16)] * 2,
        compiler_params=pltpu.CompilerParams(vmem_limit_bytes=VMEM_LIMIT),
        cost_estimate=pl.CostEstimate(
            flops=800_000_000, bytes_accessed=2_000_000, transcendentals=0
        ),
        name="combine",
    )(returned, target, mixed, gate)


def shifts(axis):
    count = lax.axis_size(axis)
    forward = [(i, i + 1) for i in range(count - 1)]
    return forward, [(target, source) for source, target in forward]


def per_device(tokens, gate, route, cotangent, w_qkv, w_proj, w_up, w_down):
    tile_rows, tile_cols, feature = tokens.shape
    tok_count = tile_rows * tile_cols
    margin = margin_cells
    experts = lax.axis_size("exp")
    capacity = max(2, 3 * tok_count // (2 * experts))
    weights = lax.all_gather(
        jnp.concatenate([w_up, w_down], axis=0), "rep", axis=0, tiled=False
    )
    forward, backward = shifts("rep")
    low = lax.ppermute(tokens[tile_rows - margin :], "rep", forward)
    high = lax.ppermute(tokens[:margin], "rep", backward)
    forward, backward = shifts("exp")

    def strip(cols):
        parts = [low[:, cols], tokens[:, cols], high[:, cols]]
        return jnp.concatenate(parts, axis=0).reshape(-1, feature)

    left = lax.ppermute(strip(slice(tile_cols - margin, tile_cols)), "exp", forward)
    right = lax.ppermute(strip(slice(0, margin)), "exp", backward)
    at = jnp.stack(
        [
            lax.axis_index("rep"),
            jnp.int32(lax.axis_size("rep")),
            lax.axis_index("exp"),
            jnp.int32(experts),
        ]
    ).astype(jnp.int32)
    gate_rows = gate.reshape(tok_count, 1)
    mixed, slots, target = front(
        at,
        tokens.reshape(tok_count, feature),
        low.reshape(-1, feature),
        high.reshape(-1, feature),
        left,
        right,
        w_qkv,
        w_proj,
        route.reshape(1, tok_count),
        gate_rows,
        cotangent.reshape(tok_count, feature),
        experts,
        capacity,
    )
    sent = lax.all_to_all(
        slots.reshape(experts, 2 * capacity, feature), "exp", 0, 0, tiled=True
    )
    slot_rows = sent[:, :capacity].reshape(-1, feature)
    slot_grads = sent[:, capacity:].reshape(-1, feature)
    grads, hidden, pre_grad = middle(weights, slot_rows, slot_grads)
    summed = lax.psum_scatter(grads, "rep", scatter_dimension=0, tiled=True)[0]
    expert_out, input_slots = back(weights, hidden, pre_grad)
    both = jnp.concatenate(
        [
            expert_out.reshape(experts, capacity, feature),
            input_slots.reshape(experts, capacity, feature),
        ],
        axis=1,
    )
    returned = lax.all_to_all(both, "exp", 0, 0, tiled=True).reshape(-1, feature)
    layer_out, input_grad = combine(returned, target, mixed, gate_rows, capacity)
    average_factor = 1.0 / lax.axis_size("rep")
    width = w_up.shape[1]
    total = summed.astype(jnp.float32) * average_factor
    return (
        layer_out.reshape(tile_rows, tile_cols, feature),
        input_grad.reshape(tile_rows, tile_cols, feature),
        total[:width][None],
        total[width:][None],
    )


def solution(mesh):
    placed = (
        P("rep", "exp", None),
        P("rep", "exp"),
        P("rep", "exp", None, None),
        P("rep", "exp", None),
        P(),
        P(),
        P("exp", "rep", None),
        P("exp", "rep", None),
    )
    return jax.shard_map(
        per_device,
        mesh=mesh,
        in_specs=placed,
        out_specs=(
            P("rep", "exp", None),
            P("rep", "exp", None),
            P("exp", "rep", None),
            P("exp", "rep", None),
        ),
        check_vma=False,
    )
```

```python
import functools
import math

import jax
import jax.numpy as jnp
import numpy as np
from jax import lax
from jax.experimental import pallas as pl
from jax.experimental.pallas import tpu as pltpu
from jax.sharding import PartitionSpec as P

HEADS = 16


GELU_C = math.sqrt(2.0 / math.pi)
window_side = 8
margin_cells = 4
CHUNKS = 4

VMEM_LIMIT = 24 * 1024 * 1024


def nt(a, b):
    return lax.dot_general(a, b, (((1,), (1,)), ((), ())), preferred_element_type=jnp.float32)


def tn(a, b):
    return lax.dot_general(a, b, (((0,), (0,)), ((), ())), preferred_element_type=jnp.float32)


def unpack_kernel(capacity, sent_ref, x_ref, g_ref):
    f32, bf16 = jnp.float32, jnp.bfloat16
    sent = sent_ref[...]
    own = sent.shape[0] // 2
    row = lax.broadcasted_iota(jnp.int32, (own, 2 * own), 0)
    expert = ((row.astype(f32) + 0.5) * (1.0 / capacity)).astype(jnp.int32)
    place = lax.broadcasted_iota(jnp.int32, (own, 2 * own), 1) - (row + capacity * expert)
    x_ref[...] = jnp.dot(
        (place == 0).astype(f32).astype(bf16), sent, preferred_element_type=f32
    ).astype(bf16)
    g_ref[...] = jnp.dot(
        (place == capacity).astype(f32).astype(bf16), sent, preferred_element_type=f32
    ).astype(bf16)


def unpack(sent, capacity):
    rows, feature = sent.shape
    vmem = pl.BlockSpec(memory_space=pltpu.VMEM)
    return pl.pallas_call(
        functools.partial(unpack_kernel, capacity),
        in_specs=[vmem],
        out_specs=[vmem] * 2,
        out_shape=[jax.ShapeDtypeStruct((rows // 2, feature), jnp.bfloat16)] * 2,
        compiler_params=pltpu.CompilerParams(vmem_limit_bytes=VMEM_LIMIT),
        cost_estimate=pl.CostEstimate(
            flops=600_000_000, bytes_accessed=1_600_000, transcendentals=0
        ),
        name="unpack",
    )(sent)


def middle_kernel(w_ref, *refs):
    slots, (grads_ref, hid_ref, pg_ref) = refs[:-3], refs[-3:]
    shards, _, width, feature = w_ref.shape
    up = w_ref[:, 0].reshape(shards * width, feature)
    down = w_ref[:, 1].reshape(shards * width, feature)
    rows = slots[0].shape[0]
    halves = len(slots) // 2
    pres = [nt(up, slots[2 * n][...]) for n in range(halves)]
    backs = [nt(down, slots[2 * n + 1][...]) for n in range(halves)]
    grad_up = grad_down = None
    for n in range(halves):
        pre = pres[n]
        square = pre * pre
        inner = jnp.tanh(pre * (GELU_C + (GELU_C * 0.044715) * square))
        half = 0.5 + 0.5 * inner
        hidden = (pre * half).astype(jnp.bfloat16)
        slope = half + (0.5 * pre) * (1.0 - inner * inner) * (
            GELU_C + (3.0 * 0.044715 * GELU_C) * square
        )
        pre_grad = (backs[n] * slope).astype(jnp.bfloat16)
        hid_ref[:, n * rows : (n + 1) * rows] = hidden
        pg_ref[:, n * rows : (n + 1) * rows] = pre_grad
        by_up = jnp.dot(pre_grad, slots[2 * n][...], preferred_element_type=jnp.float32)
        by_down = jnp.dot(hidden, slots[2 * n + 1][...], preferred_element_type=jnp.float32)
        grad_up = by_up if grad_up is None else grad_up + by_up
        grad_down = by_down if grad_down is None else grad_down + by_down
    grads_ref[:, :width] = grad_up.astype(jnp.bfloat16).reshape(shards, width, feature)
    grads_ref[:, width:] = grad_down.astype(jnp.bfloat16).reshape(shards, width, feature)


def middle(weights, slots):
    owners, _, width, feature = weights.shape
    rows = slots[0].shape[0]
    step = owners // CHUNKS
    ff = owners * width
    total = rows * len(slots) // 2
    return pl.pallas_call(
        middle_kernel,
        grid=(CHUNKS,),
        in_specs=[pl.BlockSpec((step, 2, width, feature), lambda i: (i, 0, 0, 0))]
        + [pl.BlockSpec((rows, feature), lambda i: (0, 0))] * len(slots),
        out_specs=[
            pl.BlockSpec((step, 2 * width, feature), lambda i: (i, 0, 0)),
            pl.BlockSpec((step * width, total), lambda i: (i, 0)),
            pl.BlockSpec((step * width, total), lambda i: (i, 0)),
        ],
        out_shape=[
            pltpu.HBM((owners, 2 * width, feature), jnp.bfloat16),
            pltpu.HBM((ff, total), jnp.bfloat16),
            pltpu.HBM((ff, total), jnp.bfloat16),
        ],
        compiler_params=pltpu.CompilerParams(vmem_limit_bytes=VMEM_LIMIT),
        cost_estimate=pl.CostEstimate(
            flops=8 * total * ff * feature,
            bytes_accessed=8 * ff * feature + 4 * ff * total,
            transcendentals=ff * total,
        ),
        name="middle",
    )(weights, *slots)


def back_kernel(w_ref, hid_ref, pg_ref, kept_ref, given_ref, out_acc, in_acc):
    shards, _, width, feature = w_ref.shape
    up = w_ref[:, 0].reshape(shards * width, feature)
    down = w_ref[:, 1].reshape(shards * width, feature)

    @pl.when(pl.program_id(0) == 0)
    def _():
        out_acc[...] = jnp.zeros_like(out_acc)
        in_acc[...] = jnp.zeros_like(in_acc)

    out_acc[...] += tn(hid_ref[...], down)
    in_acc[...] += tn(pg_ref[...], up)

    @pl.when(pl.program_id(0) == pl.num_programs(0) - 1)
    def _():
        own = out_acc.shape[0] // 2
        kept_ref[:own] = out_acc[:own]
        kept_ref[own:] = in_acc[:own]
        given_ref[:own] = out_acc[own:].astype(jnp.bfloat16)
        given_ref[own:] = in_acc[own:].astype(jnp.bfloat16)


def back(weights, hidden, pre_grad):
    owners, _, width, feature = weights.shape
    ff, rows = hidden.shape
    steps = 4
    step = owners // steps
    return pl.pallas_call(
        back_kernel,
        grid=(steps,),
        in_specs=[
            pl.BlockSpec((step, 2, width, feature), lambda i: (i, 0, 0, 0)),
            pl.BlockSpec((step * width, rows), lambda i: (i, 0)),
            pl.BlockSpec((step * width, rows), lambda i: (i, 0)),
        ],
        out_specs=[
            pl.BlockSpec((rows, feature), lambda i: (0, 0)),
            pl.BlockSpec((rows, feature), lambda i: (0, 0)),
        ],
        out_shape=[
            jax.ShapeDtypeStruct((rows, feature), jnp.float32),
            jax.ShapeDtypeStruct((rows, feature), jnp.bfloat16),
        ],
        scratch_shapes=[pltpu.VMEM((rows, feature), jnp.float32)] * 2,
        compiler_params=pltpu.CompilerParams(vmem_limit_bytes=VMEM_LIMIT),
        cost_estimate=pl.CostEstimate(
            flops=4 * rows * ff * feature,
            bytes_accessed=4 * ff * feature + 4 * ff * rows,
            transcendentals=0,
        ),
        name="back",
    )(weights, hidden, pre_grad)


def assemble_kernel(capacity, kept_ref, got_ref, both_ref):
    f32, bf16 = jnp.float32, jnp.bfloat16
    total = (kept_ref[...] + got_ref[...].astype(f32)).astype(bf16)
    rows = total.shape[0]
    own = rows // 2
    column = lax.broadcasted_iota(jnp.int32, (rows, own), 1)
    expert = ((column.astype(f32) + 0.5) * (1.0 / capacity)).astype(jnp.int32)
    place = lax.broadcasted_iota(jnp.int32, (rows, own), 0) - (column + capacity * expert)
    both = jnp.dot((place == 0).astype(f32).astype(bf16), total[:own], preferred_element_type=f32)
    both = both + jnp.dot(
        (place == capacity).astype(f32).astype(bf16), total[own:], preferred_element_type=f32
    )
    both_ref[...] = both.astype(bf16)


def assemble(kept, got, capacity):
    vmem = pl.BlockSpec(memory_space=pltpu.VMEM)
    return pl.pallas_call(
        functools.partial(assemble_kernel, capacity),
        in_specs=[vmem] * 2,
        out_specs=vmem,
        out_shape=jax.ShapeDtypeStruct(got.shape, jnp.bfloat16),
        compiler_params=pltpu.CompilerParams(vmem_limit_bytes=VMEM_LIMIT),
        cost_estimate=pl.CostEstimate(
            flops=800_000_000, bytes_accessed=3_000_000, transcendentals=0
        ),
        name="assemble",
    )(kept, got)


def window_rows(side, margin, tile):
    ext = tile + 2 * margin
    wins = ext // side
    edge, strip = margin * tile, ext * margin
    into = np.zeros((ext * ext, ext * ext), np.float32)
    outof = np.zeros((tile * tile, ext * ext), np.float32)
    for r in range(ext):
        for c in range(ext):
            at = ((r // side) * wins + c // side) * side * side + (r % side) * side + c % side
            base = tile * tile
            if c < margin:
                piece = base + 2 * edge + r * margin + c
            elif c >= tile + margin:
                piece = base + 2 * edge + strip + r * margin + c - tile - margin
            elif r < margin:
                piece = base + r * tile + c - margin
            elif r >= tile + margin:
                piece = base + edge + (r - tile - margin) * tile + c - margin
            else:
                piece = (r - margin) * tile + c - margin
                outof[piece, at] = 1.0
            into[at, piece] = 1.0
    return into.astype(jnp.bfloat16), outof.astype(jnp.bfloat16)


def placers(target, slots, capacity):
    rows = lax.broadcasted_iota(jnp.int32, (2 * slots, target.shape[1]), 0)
    return rows == target, rows == target + capacity


def front_kernel(
    experts, capacity, at_ref, tok_ref, low_ref, high_ref, left_ref, right_ref, into_ref, outof_ref,
    wqkv_ref, wproj_ref, route_ref, gate_ref, cot_ref, mixed_ref, slots_ref, target_ref, qkv_ref, ctx_ref,
):
    bf16, f32 = jnp.bfloat16, jnp.float32
    tokens = tok_ref[...]
    count, feature = tokens.shape
    cells = window_side * window_side
    head = feature // HEADS
    group = 128 // head
    pieces = jnp.concatenate(
        [tokens, low_ref[...], high_ref[...], left_ref[...], right_ref[...]], axis=0
    )
    placed = jnp.dot(into_ref[...], pieces, preferred_element_type=f32).astype(bf16)
    qkv_ref[...] = jnp.dot(placed, wqkv_ref[...], preferred_element_type=f32).astype(bf16)
    first_row, last_row = at_ref[0] == 0, at_ref[0] == at_ref[1] - 1
    first_col, last_col = at_ref[2] == 0, at_ref[2] == at_ref[3] - 1
    lane = lax.broadcasted_iota(jnp.int32, (1, 128), 1)
    own = [
        ((lane >= h * head) & (lane < (h + 1) * head)).astype(f32) for h in range(group)
    ]
    own16 = [o.astype(bf16) for o in own]
    key = lax.broadcasted_iota(jnp.int32, (cells, 128), 0)
    key_row, key_col = key // window_side, key % window_side
    half = window_side // 2
    low_bias = jnp.float32(-1e30)
    edge_bias = {
        (0, 0): jnp.where(key_row < half, jnp.where(first_row, low_bias, 0.0), 0.0),
        (0, 2): jnp.where(key_row >= half, jnp.where(last_row, low_bias, 0.0), 0.0),
        (1, 0): jnp.where(key_col < half, jnp.where(first_col, low_bias, 0.0), 0.0),
        (1, 2): jnp.where(key_col >= half, jnp.where(last_col, low_bias, 0.0), 0.0),
    }
    scale = 1.0 / math.sqrt(head)
    for window in range(9):
        wi, wj = window // 3, window % 3
        bias = None
        if wi != 1:
            bias = edge_bias[0, wi]
        if wj != 1:
            bias = edge_bias[1, wj] if bias is None else bias + edge_bias[1, wj]
        if bias is not None:
            bias = jnp.concatenate([bias] * (group * cells // 128), axis=1)
        rows = slice(window * cells, (window + 1) * cells)
        for g in range(feature // 128):
            q = qkv_ref[rows, g * 128 : (g + 1) * 128]
            k = qkv_ref[rows, feature + g * 128 : feature + (g + 1) * 128]
            v = qkv_ref[rows, 2 * feature + g * 128 : 2 * feature + (g + 1) * 128]
            spread = jnp.concatenate([q * o for o in own16], axis=0)
            scores = nt(k, spread)
            if bias is not None:
                scores = scores + bias
            peak = jnp.max(scores, axis=0, keepdims=True)
            weights = jnp.exp((scores - peak) * scale)
            probs = (weights * (1.0 / jnp.sum(weights, axis=0, keepdims=True))).astype(bf16)
            wide = tn(probs, v)
            mine = wide[:cells] * own[0]
            for h in range(1, group):
                mine = mine + wide[h * cells : (h + 1) * cells] * own[h]
            ctx_ref[rows, g * 128 : (g + 1) * 128] = mine.astype(bf16)
    context = jnp.dot(outof_ref[...], ctx_ref[...], preferred_element_type=f32).astype(bf16)
    attended = jnp.dot(context, wproj_ref[...], preferred_element_type=f32)
    centred = attended - jnp.mean(attended, axis=-1, keepdims=True)
    spread_of = jnp.mean(centred * centred, axis=-1, keepdims=True)
    mixed = (tokens.astype(f32) + centred * lax.rsqrt(spread_of + 1e-05)).astype(bf16)
    mixed_ref[...] = mixed
    route = route_ref[...]
    matches = lax.broadcasted_iota(jnp.int32, (experts, count), 0) == route
    matches = matches.astype(f32)
    earlier = lax.broadcasted_iota(jnp.int32, (count, count), 0) < lax.broadcasted_iota(
        jnp.int32, (count, count), 1
    )
    before = jnp.dot(
        matches.astype(bf16), earlier.astype(f32).astype(bf16), preferred_element_type=f32
    )
    position = jnp.sum(matches * before, axis=0, keepdims=True).astype(jnp.int32)
    target = route * (2 * capacity) + position
    target_ref[...] = target
    upstream = (gate_ref[...] * cot_ref[...].astype(f32)).astype(bf16)
    place_x, place_g = placers(target, experts * capacity, capacity)
    slots = jnp.dot(place_x.astype(f32).astype(bf16), mixed, preferred_element_type=f32)
    slots = slots + jnp.dot(
        place_g.astype(f32).astype(bf16), upstream, preferred_element_type=f32
    )
    slots_ref[...] = slots.astype(bf16)


def front(at, tokens, low, high, left, right, w_qkv, w_proj, route, gate, cotangent, experts, capacity):
    count, feature = tokens.shape
    into, outof = window_rows(window_side, margin_cells, math.isqrt(count))
    ext = into.shape[0]
    vmem = pl.BlockSpec(memory_space=pltpu.VMEM)
    return pl.pallas_call(
        functools.partial(front_kernel, experts, capacity),
        in_specs=[pl.BlockSpec(memory_space=pltpu.SMEM)] + [vmem] * 12,
        out_specs=[vmem] * 3,
        out_shape=[
            jax.ShapeDtypeStruct((count, feature), jnp.bfloat16),
            jax.ShapeDtypeStruct((2 * experts * capacity, feature), jnp.bfloat16),
            jax.ShapeDtypeStruct((1, count), jnp.int32),
        ],
        scratch_shapes=[
            pltpu.VMEM((ext, 3 * feature), jnp.bfloat16),
            pltpu.VMEM((ext, feature), jnp.bfloat16),
        ],
        compiler_params=pltpu.CompilerParams(vmem_limit_bytes=VMEM_LIMIT),
        cost_estimate=pl.CostEstimate(
            flops=5_000_000_000, bytes_accessed=8_000_000, transcendentals=600_000
        ),
        name="front",
    )(
        at, tokens, low, high, left, right, jnp.asarray(into), jnp.asarray(outof),
        w_qkv, w_proj, route, gate, cotangent,
    )


def combine_kernel(capacity, back_ref, target_ref, mixed_ref, gate_ref, out_ref, grad_ref):
    f32 = jnp.float32
    back_rows = back_ref[...]
    place_x, place_g = placers(target_ref[...], back_rows.shape[0] // 2, capacity)
    token_out = tn(place_x.astype(f32).astype(jnp.bfloat16), back_rows)
    out_ref[...] = (mixed_ref[...].astype(f32) + gate_ref[...] * token_out).astype(jnp.bfloat16)
    grad_ref[...] = tn(place_g.astype(f32).astype(jnp.bfloat16), back_rows).astype(jnp.bfloat16)


def combine(returned, target, mixed, gate, capacity):
    vmem = pl.BlockSpec(memory_space=pltpu.VMEM)
    return pl.pallas_call(
        functools.partial(combine_kernel, capacity),
        in_specs=[vmem] * 4,
        out_specs=[vmem] * 2,
        out_shape=[jax.ShapeDtypeStruct(mixed.shape, jnp.bfloat16)] * 2,
        compiler_params=pltpu.CompilerParams(vmem_limit_bytes=VMEM_LIMIT),
        cost_estimate=pl.CostEstimate(
            flops=800_000_000, bytes_accessed=2_000_000, transcendentals=0
        ),
        name="combine",
    )(returned, target, mixed, gate)


def shifts(axis):
    count = lax.axis_size(axis)
    forward = [(i, i + 1) for i in range(count - 1)]
    return forward, [(target, source) for source, target in forward]


def sharing(axis):
    count = lax.axis_size(axis)
    groups = [list(range(parity, count, 2)) for parity in range(2)]
    return groups, [(i, i ^ 1) for i in range(count)]


def per_device(tokens, gate, route, cotangent, w_qkv, w_proj, w_up, w_down):
    tile_rows, tile_cols, feature = tokens.shape
    tok_count = tile_rows * tile_cols
    margin = margin_cells
    experts = lax.axis_size("exp")
    capacity = max(2, 3 * tok_count // (2 * experts))
    groups, swap = sharing("rep")
    weights = lax.all_gather(
        jnp.concatenate([w_up, w_down], axis=0),
        "rep",
        axis=0,
        tiled=False,
        axis_index_groups=groups,
    )
    forward, backward = shifts("rep")
    low = lax.ppermute(tokens[tile_rows - margin :], "rep", forward)
    high = lax.ppermute(tokens[:margin], "rep", backward)
    forward, backward = shifts("exp")

    def strip(cols):
        parts = [low[:, cols], tokens[:, cols], high[:, cols]]
        return jnp.concatenate(parts, axis=0).reshape(-1, feature)

    left = lax.ppermute(strip(slice(tile_cols - margin, tile_cols)), "exp", forward)
    right = lax.ppermute(strip(slice(0, margin)), "exp", backward)
    at = jnp.stack(
        [
            lax.axis_index("rep"),
            jnp.int32(lax.axis_size("rep")),
            lax.axis_index("exp"),
            jnp.int32(experts),
        ]
    ).astype(jnp.int32)
    gate_rows = gate.reshape(tok_count, 1)
    mixed, slots, target = front(
        at,
        tokens.reshape(tok_count, feature),
        low.reshape(-1, feature),
        high.reshape(-1, feature),
        left,
        right,
        w_qkv,
        w_proj,
        route.reshape(1, tok_count),
        gate_rows,
        cotangent.reshape(tok_count, feature),
        experts,
        capacity,
    )
    sent = lax.all_to_all(
        slots.reshape(experts, 2 * capacity, feature), "exp", 0, 0, tiled=True
    )
    sent = sent.reshape(-1, feature)
    other = lax.ppermute(sent, "rep", swap)
    slot_parts = [*unpack(sent, capacity), *unpack(other, capacity)]
    grads, hidden, pre_grad = middle(weights, slot_parts)
    summed = lax.psum_scatter(
        grads, "rep", scatter_dimension=0, tiled=True, axis_index_groups=groups
    )[0]
    kept, given = back(weights, hidden, pre_grad)
    both = assemble(kept, lax.ppermute(given, "rep", swap), capacity)
    returned = lax.all_to_all(
        both.reshape(experts, 2 * capacity, feature), "exp", 0, 0, tiled=True
    ).reshape(-1, feature)
    layer_out, input_grad = combine(returned, target, mixed, gate_rows, capacity)
    average_factor = 1.0 / lax.axis_size("rep")
    width = w_up.shape[1]
    total = summed.astype(jnp.float32) * average_factor
    return (
        layer_out.reshape(tile_rows, tile_cols, feature),
        input_grad.reshape(tile_rows, tile_cols, feature),
        total[:width][None],
        total[width:][None],
    )


def solution(mesh):
    placed = (
        P("rep", "exp", None),
        P("rep", "exp"),
        P("rep", "exp", None, None),
        P("rep", "exp", None),
        P(),
        P(),
        P("exp", "rep", None),
        P("exp", "rep", None),
    )
    return jax.shard_map(
        per_device,
        mesh=mesh,
        in_specs=placed,
        out_specs=(
            P("rep", "exp", None),
            P("rep", "exp", None),
            P("exp", "rep", None),
            P("exp", "rep", None),
        ),
        check_vma=False,
    )
```

```python
import functools
import math

import jax
import jax.numpy as jnp
from jax import lax
from jax.experimental import pallas as pl
from jax.experimental.pallas import tpu as pltpu
from jax.sharding import PartitionSpec as P

HEADS = 16


GELU_C = math.sqrt(2.0 / math.pi)
window_side = 8
margin_cells = 4
CHUNKS = 4
EXTRA = 16

VMEM_LIMIT = 24 * 1024 * 1024
MIDDLE_LIMIT = 58 * 1024 * 1024


def nt(a, b):
    return lax.dot_general(a, b, (((1,), (1,)), ((), ())), preferred_element_type=jnp.float32)


def tn(a, b):
    return lax.dot_general(a, b, (((0,), (0,)), ((), ())), preferred_element_type=jnp.float32)


def nn(a, b):
    return jnp.dot(a, b, preferred_element_type=jnp.float32)


def one_hot(mask):
    return mask.astype(jnp.float32).astype(jnp.bfloat16)


def vmem_call(kernel, out, name, flops, in_specs=None, count=0, **more):
    vmem = pl.BlockSpec(memory_space=pltpu.VMEM)
    return pl.pallas_call(
        kernel,
        in_specs=in_specs or [vmem] * count,
        out_specs=[vmem] * len(out),
        out_shape=[jax.ShapeDtypeStruct(shape, dtype) for shape, dtype in out],
        compiler_params=pltpu.CompilerParams(vmem_limit_bytes=VMEM_LIMIT),
        cost_estimate=pl.CostEstimate(flops=flops, bytes_accessed=3_000_000, transcendentals=0),
        name=name,
        **more,
    )


def upstream_kernel(route_ref, gate_ref, cot_ref, give_ref):
    f32, bf16 = jnp.float32, jnp.bfloat16
    count, feature = cot_ref.shape
    give_ref[:count] = (gate_ref[...] * cot_ref[...].astype(f32)).astype(bf16)
    route = route_ref[...].astype(f32)
    row = jnp.concatenate([route, jnp.zeros((1, feature - count), f32)], axis=1)
    extra = give_ref.shape[0] - count
    give_ref[count:] = jnp.broadcast_to(row, (extra, feature)).astype(bf16)


def slot_numbers(route, experts):
    count = route.shape[1]
    matches = lax.broadcasted_iota(jnp.int32, (experts, count), 0) == route
    earlier = lax.broadcasted_iota(jnp.int32, (count, count), 0) < lax.broadcasted_iota(
        jnp.int32, (count, count), 1
    )
    before = nn(one_hot(matches), one_hot(earlier))
    return jnp.sum(jnp.where(matches, before, 0.0), axis=0, keepdims=True).astype(jnp.int32)


def placer(target, rows):
    return one_hot(lax.broadcasted_iota(jnp.int32, (rows, target.shape[1]), 0) == target)


def grad_slots_kernel(experts, capacity, give_ref, got_ref, slots_ref, target_ref):
    feature = give_ref.shape[1]
    count = give_ref.shape[0] - EXTRA
    total = None
    for n, ref in enumerate((give_ref, got_ref)):
        route = ref[count:, :count].astype(jnp.float32)[:1].astype(jnp.int32)
        target = route * (2 * capacity) + n * capacity + slot_numbers(route, experts)
        target_ref[n : n + 1] = target
        placed = nn(placer(target, 2 * experts * capacity), ref[:count])
        total = placed if total is None else total + placed
    slots_ref[...] = total.astype(jnp.bfloat16)


def token_slots_kernel(target_ref, mixed_ref, got_ref, slots_ref):
    rows = slots_ref.shape[0]
    total = nn(placer(target_ref[0:1], rows), mixed_ref[...])
    total = total + nn(placer(target_ref[1:2], rows), got_ref[...])
    slots_ref[...] = total.astype(jnp.bfloat16)


def back_rows_kernel(target_ref, back_ref, give_ref):
    give_ref[...] = tn(placer(target_ref[1:2], back_ref.shape[0]), back_ref[...]).astype(
        jnp.bfloat16
    )


def combine_kernel(
    target_ref, out_ref, got_out_ref, in_ref, got_in_ref, mixed_ref, gate_ref, layer_ref, grad_ref
):
    f32, bf16 = jnp.float32, jnp.bfloat16
    mine = placer(target_ref[0:1], out_ref.shape[0])
    token_out = tn(mine, out_ref[...]) + got_out_ref[...].astype(f32)
    layer_ref[...] = (mixed_ref[...].astype(f32) + gate_ref[...] * token_out).astype(bf16)
    grad_ref[...] = (tn(mine, in_ref[...]) + got_in_ref[...].astype(f32)).astype(bf16)


def gradients_kernel(scale, sum_ref, up_ref, down_ref):
    width = up_ref.shape[1]
    up_ref[0] = sum_ref[0, :width].astype(jnp.float32) * scale
    down_ref[0] = sum_ref[0, width:].astype(jnp.float32) * scale


def middle_kernel(w_hbm, x_ref, g_ref, grads_ref, hid_ref, pg_ref, w_ref, sems):
    step = pl.program_id(0)
    shards = w_ref.shape[1]
    copies = [
        pltpu.make_async_copy(w_hbm.at[pl.ds(n * shards, shards)], w_ref.at[n], sems.at[n])
        for n in range(CHUNKS)
    ]

    @pl.when(step == 0)
    def _():
        for copy in copies:
            copy.start()

    for n in range(CHUNKS):

        @pl.when(step == n)
        def _():
            copies[n].wait()

    held = w_ref[step]
    _, _, width, feature = held.shape
    up = held[:, 0].reshape(shards * width, feature)
    down = held[:, 1].reshape(shards * width, feature)
    halves = 2
    rows = x_ref.shape[0] // halves
    parts = [slice(n * rows, (n + 1) * rows) for n in range(halves)]
    pres = [nt(up, x_ref[part]) for part in parts]
    backs = [nt(down, g_ref[part]) for part in parts]
    grad_up = grad_down = None
    for n, part in enumerate(parts):
        pre = pres[n]
        square = pre * pre
        inner = jnp.tanh(pre * (GELU_C + (GELU_C * 0.044715) * square))
        half = 0.5 + 0.5 * inner
        hidden = (pre * half).astype(jnp.bfloat16)
        slope = half + (0.5 * pre) * (1.0 - inner * inner) * (
            GELU_C + (3.0 * 0.044715 * GELU_C) * square
        )
        pre_grad = (backs[n] * slope).astype(jnp.bfloat16)
        hid_ref[:, part] = hidden
        pg_ref[:, part] = pre_grad
        by_up = nn(pre_grad, x_ref[part])
        by_down = nn(hidden, g_ref[part])
        grad_up = by_up if grad_up is None else grad_up + by_up
        grad_down = by_down if grad_down is None else grad_down + by_down
    grads_ref[:, :width] = grad_up.astype(jnp.bfloat16).reshape(shards, width, feature)
    grads_ref[:, width:] = grad_down.astype(jnp.bfloat16).reshape(shards, width, feature)


def middle(weights, slot_x, slot_g):
    owners, _, width, feature = weights.shape
    rows = slot_x.shape[0]
    step = owners // CHUNKS
    ff = owners * width
    return pl.pallas_call(
        middle_kernel,
        grid=(CHUNKS,),
        in_specs=[
            pl.BlockSpec(memory_space=pltpu.HBM),
            pl.BlockSpec((rows, feature), lambda i: (0, 0)),
            pl.BlockSpec((rows, feature), lambda i: (0, 0)),
        ],
        out_specs=[
            pl.BlockSpec((step, 2 * width, feature), lambda i: (i, 0, 0)),
            pl.BlockSpec((step * width, rows), lambda i: (i, 0)),
            pl.BlockSpec((step * width, rows), lambda i: (i, 0)),
        ],
        out_shape=[
            pltpu.HBM((owners, 2 * width, feature), jnp.bfloat16),
            pltpu.HBM((ff, rows), jnp.bfloat16),
            pltpu.HBM((ff, rows), jnp.bfloat16),
        ],
        scratch_shapes=[
            pltpu.VMEM((CHUNKS, step, 2, width, feature), jnp.bfloat16),
            pltpu.SemaphoreType.DMA((CHUNKS,)),
        ],
        compiler_params=pltpu.CompilerParams(vmem_limit_bytes=MIDDLE_LIMIT),
        cost_estimate=pl.CostEstimate(
            flops=8 * rows * ff * feature,
            bytes_accessed=8 * ff * feature + 4 * ff * rows,
            transcendentals=ff * rows,
        ),
        name="middle",
    )(weights, slot_x, slot_g)


def back_kernel(side, w_ref, act_ref, out_ref, acc):
    shards, _, width, feature = w_ref.shape
    matrix = w_ref[:, 0].reshape(shards * width, feature)

    @pl.when(pl.program_id(0) == 0)
    def _():
        acc[...] = jnp.zeros_like(acc)

    acc[...] += tn(act_ref[...], matrix)

    @pl.when(pl.program_id(0) == pl.num_programs(0) - 1)
    def _():
        out_ref[...] = acc[...].astype(jnp.bfloat16)


def back(weights, activity, side):
    owners, _, width, feature = weights.shape
    ff, rows = activity.shape
    steps = 2
    step = owners // steps
    return pl.pallas_call(
        functools.partial(back_kernel, side),
        grid=(steps,),
        in_specs=[
            pl.BlockSpec((step, 1, width, feature), lambda i: (i, side, 0, 0)),
            pl.BlockSpec((step * width, rows), lambda i: (i, 0)),
        ],
        out_specs=pl.BlockSpec((rows, feature), lambda i: (0, 0)),
        out_shape=jax.ShapeDtypeStruct((rows, feature), jnp.bfloat16),
        scratch_shapes=[pltpu.VMEM((rows, feature), jnp.float32)],
        compiler_params=pltpu.CompilerParams(vmem_limit_bytes=VMEM_LIMIT),
        cost_estimate=pl.CostEstimate(
            flops=2 * rows * ff * feature,
            bytes_accessed=2 * ff * feature + 2 * ff * rows,
            transcendentals=0,
        ),
        name="back",
    )(weights, activity)


def window_index(row, col, tile):
    wins = (tile + 2 * margin_cells) // window_side
    window = (row // window_side) * wins + col // window_side
    return (window * window_side + row % window_side) * window_side + col % window_side


def into_windows(tile):
    ext = tile + 2 * margin_cells
    edge, strip = margin_cells * tile, margin_cells * ext
    piece = lax.broadcasted_iota(jnp.int32, (1, ext * ext), 1)
    base = tile * tile
    row, col = margin_cells + piece // tile, margin_cells + piece % tile
    low = piece - base
    row = jnp.where(piece >= base, low // tile, row)
    high = piece - (base + edge)
    row = jnp.where(piece >= base + edge, tile + margin_cells + high // tile, row)
    left = piece - (base + 2 * edge)
    side = piece >= base + 2 * edge
    row = jnp.where(side, left // margin_cells, row)
    col = jnp.where(side, left % margin_cells, col)
    right = left - strip
    side = piece >= base + 2 * edge + strip
    row = jnp.where(side, right // margin_cells, row)
    col = jnp.where(side, tile + margin_cells + right % margin_cells, col)
    place = window_index(row, col, tile)
    return one_hot(lax.broadcasted_iota(jnp.int32, (ext * ext, ext * ext), 0) == place)


def out_of_windows(tile):
    ext = tile + 2 * margin_cells
    token = lax.broadcasted_iota(jnp.int32, (tile * tile, 1), 0)
    place = window_index(token // tile + margin_cells, token % tile + margin_cells, tile)
    return one_hot(lax.broadcasted_iota(jnp.int32, (tile * tile, ext * ext), 1) == place)


def front_kernel(
    at_ref, tok_ref, low_ref, high_ref, left_ref, right_ref, wqkv_ref, wproj_ref, mixed_ref, qkv_ref, ctx_ref
):
    bf16, f32 = jnp.bfloat16, jnp.float32
    tokens = tok_ref[...]
    count, feature = tokens.shape
    cells = window_side * window_side
    head = feature // HEADS
    group = 128 // head
    pieces = jnp.concatenate(
        [tokens, low_ref[...], high_ref[...], left_ref[...], right_ref[...]], axis=0
    )
    placed = nn(into_windows(math.isqrt(count)), pieces).astype(bf16)
    qkv_ref[...] = jnp.dot(placed, wqkv_ref[...], preferred_element_type=f32).astype(bf16)
    first_row, last_row = at_ref[0] == 0, at_ref[0] == at_ref[1] - 1
    first_col, last_col = at_ref[2] == 0, at_ref[2] == at_ref[3] - 1
    lane = lax.broadcasted_iota(jnp.int32, (1, 128), 1)
    own = [
        ((lane >= h * head) & (lane < (h + 1) * head)).astype(f32) for h in range(group)
    ]
    own16 = [o.astype(bf16) for o in own]
    key = lax.broadcasted_iota(jnp.int32, (cells, 128), 0)
    key_row, key_col = key // window_side, key % window_side
    half = window_side // 2
    low_bias = jnp.float32(-1e30)
    edge_bias = {
        (0, 0): jnp.where(key_row < half, jnp.where(first_row, low_bias, 0.0), 0.0),
        (0, 2): jnp.where(key_row >= half, jnp.where(last_row, low_bias, 0.0), 0.0),
        (1, 0): jnp.where(key_col < half, jnp.where(first_col, low_bias, 0.0), 0.0),
        (1, 2): jnp.where(key_col >= half, jnp.where(last_col, low_bias, 0.0), 0.0),
    }
    scale = 1.0 / math.sqrt(head)
    for window in range(9):
        wi, wj = window // 3, window % 3
        bias = None
        if wi != 1:
            bias = edge_bias[0, wi]
        if wj != 1:
            bias = edge_bias[1, wj] if bias is None else bias + edge_bias[1, wj]
        if bias is not None:
            bias = jnp.concatenate([bias] * (group * cells // 128), axis=1)
        rows = slice(window * cells, (window + 1) * cells)
        for g in range(feature // 128):
            q = qkv_ref[rows, g * 128 : (g + 1) * 128]
            k = qkv_ref[rows, feature + g * 128 : feature + (g + 1) * 128]
            v = qkv_ref[rows, 2 * feature + g * 128 : 2 * feature + (g + 1) * 128]
            spread = jnp.concatenate([q * o for o in own16], axis=0)
            scores = nt(k, spread)
            if bias is not None:
                scores = scores + bias
            peak = jnp.max(scores, axis=0, keepdims=True)
            weights = jnp.exp((scores - peak) * scale)
            probs = (weights * (1.0 / jnp.sum(weights, axis=0, keepdims=True))).astype(bf16)
            wide = tn(probs, v)
            mine = wide[:cells] * own[0]
            for h in range(1, group):
                mine = mine + wide[h * cells : (h + 1) * cells] * own[h]
            ctx_ref[rows, g * 128 : (g + 1) * 128] = mine.astype(bf16)
    context = nn(out_of_windows(math.isqrt(count)), ctx_ref[...]).astype(bf16)
    attended = jnp.dot(context, wproj_ref[...], preferred_element_type=f32)
    centred = attended - jnp.mean(attended, axis=-1, keepdims=True)
    spread_of = jnp.mean(centred * centred, axis=-1, keepdims=True)
    mixed = (tokens.astype(f32) + centred * lax.rsqrt(spread_of + 1e-05)).astype(bf16)
    mixed_ref[...] = mixed


def front(at, tokens, low, high, left, right, w_qkv, w_proj):
    count, feature = tokens.shape
    ext = (math.isqrt(count) + 2 * margin_cells) ** 2
    smem = pl.BlockSpec(memory_space=pltpu.SMEM)
    vmem = pl.BlockSpec(memory_space=pltpu.VMEM)
    return vmem_call(
        front_kernel,
        [((count, feature), jnp.bfloat16)],
        "front",
        4_000_000_000,
        in_specs=[smem] + [vmem] * 7,
        scratch_shapes=[
            pltpu.VMEM((ext, 3 * feature), jnp.bfloat16),
            pltpu.VMEM((ext, feature), jnp.bfloat16),
        ],
    )(at, tokens, low, high, left, right, w_qkv, w_proj)[0]


def shifts(axis):
    count = lax.axis_size(axis)
    forward = [(i, i + 1) for i in range(count - 1)]
    return forward, [(target, source) for source, target in forward]


def sharing(axis):
    count = lax.axis_size(axis)
    groups = [list(range(parity, count, 2)) for parity in range(2)]
    return groups, [(i, i ^ 1) for i in range(count)]


def per_device(tokens, gate, route, cotangent, w_qkv, w_proj, w_up, w_down):
    tile_rows, tile_cols, feature = tokens.shape
    tok_count = tile_rows * tile_cols
    margin = margin_cells
    experts = lax.axis_size("exp")
    capacity = max(2, 3 * tok_count // (2 * experts))
    slot_count = 2 * experts * capacity
    bf16, f32 = jnp.bfloat16, jnp.float32
    rows_of = ((slot_count, feature), bf16)
    groups, swap = sharing("rep")

    def dispatch(rows):
        blocks = rows.reshape(experts, -1, feature)
        return lax.all_to_all(blocks, "exp", 0, 0, tiled=True).reshape(-1, feature)

    weights = lax.all_gather(
        jnp.concatenate([w_up, w_down], axis=0),
        "rep",
        axis=0,
        tiled=False,
        axis_index_groups=groups,
    )
    forward, backward = shifts("rep")
    low = lax.ppermute(tokens[tile_rows - margin :], "rep", forward)
    high = lax.ppermute(tokens[:margin], "rep", backward)
    gate_rows = gate.reshape(tok_count, 1)
    [give] = vmem_call(
        upstream_kernel, [((tok_count + EXTRA, feature), bf16)], "upstream", 1_000_000, count=3
    )(route.reshape(1, tok_count), gate_rows, cotangent.reshape(tok_count, feature))
    got = lax.ppermute(give, "rep", swap)
    forward, backward = shifts("exp")

    def strip(cols):
        parts = [low[:, cols], tokens[:, cols], high[:, cols]]
        return jnp.concatenate(parts, axis=0).reshape(-1, feature)

    left = lax.ppermute(strip(slice(tile_cols - margin, tile_cols)), "exp", forward)
    right = lax.ppermute(strip(slice(0, margin)), "exp", backward)
    at = jnp.stack(
        [
            lax.axis_index("rep"),
            jnp.int32(lax.axis_size("rep")),
            lax.axis_index("exp"),
            jnp.int32(experts),
        ]
    ).astype(jnp.int32)
    mixed = front(
        at,
        tokens.reshape(tok_count, feature),
        low.reshape(-1, feature),
        high.reshape(-1, feature),
        left,
        right,
        w_qkv,
        w_proj,
    )
    got_mixed = lax.ppermute(mixed, "rep", swap)
    slots_g, target = vmem_call(
        functools.partial(grad_slots_kernel, experts, capacity),
        [rows_of, ((2, tok_count), jnp.int32)],
        "grad_slots",
        500_000_000,
        count=2,
    )(give, got)
    slot_g = dispatch(slots_g)
    [slots_x] = vmem_call(token_slots_kernel, [rows_of], "token_slots", 400_000_000, count=3)(
        target, mixed, got_mixed
    )
    slot_x = dispatch(slots_x)
    grads, hidden, pre_grad = middle(weights, slot_x, slot_g)
    summed = lax.psum_scatter(
        grads, "rep", scatter_dimension=0, tiled=True, axis_index_groups=groups
    )

    def returned(activity, side):
        rows = dispatch(back(weights, activity, side))
        [theirs] = vmem_call(
            back_rows_kernel, [((tok_count, feature), bf16)], "back_rows", 200_000_000, count=2
        )(target, rows)
        return rows, lax.ppermute(theirs, "rep", swap)

    layer_out, input_grad = vmem_call(
        combine_kernel, [((tok_count, feature), bf16)] * 2, "combine", 400_000_000, count=7
    )(target, *returned(hidden, 1), *returned(pre_grad, 0), mixed, gate_rows)
    grad_up, grad_down = vmem_call(
        functools.partial(gradients_kernel, 1.0 / lax.axis_size("rep")),
        [(w_up.shape, f32)] * 2,
        "gradients",
        1_000_000,
        count=1,
    )(summed)
    return (
        layer_out.reshape(tile_rows, tile_cols, feature),
        input_grad.reshape(tile_rows, tile_cols, feature),
        grad_up,
        grad_down,
    )


def solution(mesh):
    placed = (
        P("rep", "exp", None),
        P("rep", "exp"),
        P("rep", "exp", None, None),
        P("rep", "exp", None),
        P(),
        P(),
        P("exp", "rep", None),
        P("exp", "rep", None),
    )
    return jax.shard_map(
        per_device,
        mesh=mesh,
        in_specs=placed,
        out_specs=(
            P("rep", "exp", None),
            P("rep", "exp", None),
            P("exp", "rep", None),
            P("exp", "rep", None),
        ),
        check_vma=False,
    )
```

```python
import functools
import math

import jax
import jax.numpy as jnp
from jax import lax
from jax.experimental import pallas as pl
from jax.experimental.pallas import tpu as pltpu
from jax.sharding import PartitionSpec as P

HEADS = 16


GELU_C = math.sqrt(2.0 / math.pi)
window_side = 8
margin_cells = 4
CHUNKS = 4
EXTRA = 16

VMEM_LIMIT = 24 * 1024 * 1024
MIDDLE_LIMIT = 58 * 1024 * 1024


def nt(a, b):
    return lax.dot_general(a, b, (((1,), (1,)), ((), ())), preferred_element_type=jnp.float32)


def tn(a, b):
    return lax.dot_general(a, b, (((0,), (0,)), ((), ())), preferred_element_type=jnp.float32)


def nn(a, b):
    return jnp.dot(a, b, preferred_element_type=jnp.float32)


def one_hot(mask):
    return mask.astype(jnp.float32).astype(jnp.bfloat16)


def vmem_call(kernel, out, name, flops, in_specs=None, count=0, **more):
    vmem = pl.BlockSpec(memory_space=pltpu.VMEM)
    return pl.pallas_call(
        kernel,
        in_specs=in_specs or [vmem] * count,
        out_specs=[vmem] * len(out),
        out_shape=[jax.ShapeDtypeStruct(shape, dtype) for shape, dtype in out],
        compiler_params=pltpu.CompilerParams(vmem_limit_bytes=VMEM_LIMIT),
        cost_estimate=pl.CostEstimate(flops=flops, bytes_accessed=3_000_000, transcendentals=0),
        name=name,
        **more,
    )


def upstream_kernel(route_ref, gate_ref, cot_ref, give_ref):
    f32, bf16 = jnp.float32, jnp.bfloat16
    count, feature = cot_ref.shape
    give_ref[:count] = (gate_ref[...] * cot_ref[...].astype(f32)).astype(bf16)
    route = route_ref[...].astype(f32)
    row = jnp.concatenate([route, jnp.zeros((1, feature - count), f32)], axis=1)
    extra = give_ref.shape[0] - count
    give_ref[count:] = jnp.broadcast_to(row, (extra, feature)).astype(bf16)


def slot_numbers(route, experts):
    count = route.shape[1]
    matches = lax.broadcasted_iota(jnp.int32, (experts, count), 0) == route
    earlier = lax.broadcasted_iota(jnp.int32, (count, count), 0) < lax.broadcasted_iota(
        jnp.int32, (count, count), 1
    )
    before = nn(one_hot(matches), one_hot(earlier))
    return jnp.sum(jnp.where(matches, before, 0.0), axis=0, keepdims=True).astype(jnp.int32)


def placer(target, rows):
    return one_hot(lax.broadcasted_iota(jnp.int32, (rows, target.shape[1]), 0) == target)


def grad_slots_kernel(experts, capacity, give_ref, got_ref, slots_ref, target_ref):
    feature = give_ref.shape[1]
    count = give_ref.shape[0] - EXTRA
    total = None
    for n, ref in enumerate((give_ref, got_ref)):
        route = ref[count:, :count].astype(jnp.float32)[:1].astype(jnp.int32)
        target = route * (2 * capacity) + n * capacity + slot_numbers(route, experts)
        target_ref[n : n + 1] = target
        placed = nn(placer(target, 2 * experts * capacity), ref[:count])
        total = placed if total is None else total + placed
    slots_ref[...] = total.astype(jnp.bfloat16)


def back_rows_kernel(target_ref, back_ref, give_ref):
    give_ref[...] = tn(placer(target_ref[1:2], back_ref.shape[0]), back_ref[...]).astype(
        jnp.bfloat16
    )


def combine_kernel(
    target_ref, out_ref, got_out_ref, in_ref, got_in_ref, mixed_ref, gate_ref, layer_ref, grad_ref
):
    f32, bf16 = jnp.float32, jnp.bfloat16
    mine = placer(target_ref[0:1], out_ref.shape[0])
    token_out = tn(mine, out_ref[...]) + got_out_ref[...].astype(f32)
    layer_ref[...] = (mixed_ref[...].astype(f32) + gate_ref[...] * token_out).astype(bf16)
    grad_ref[...] = (tn(mine, in_ref[...]) + got_in_ref[...].astype(f32)).astype(bf16)


def gradients_kernel(scale, sum_ref, up_ref, down_ref):
    width = up_ref.shape[1]
    up_ref[0] = sum_ref[0, :width].astype(jnp.float32) * scale
    down_ref[0] = sum_ref[0, width:].astype(jnp.float32) * scale


def middle_kernel(w_ref, x_ref, g_ref, grads_ref, hid_ref, pg_ref):
    shards, _, width, feature = w_ref.shape
    up = w_ref[:, 0].reshape(shards * width, feature)
    down = w_ref[:, 1].reshape(shards * width, feature)
    halves = 2
    rows = x_ref.shape[0] // halves
    parts = [slice(n * rows, (n + 1) * rows) for n in range(halves)]
    pres = [nt(up, x_ref[part]) for part in parts]
    backs = [nt(down, g_ref[part]) for part in parts]
    grad_up = grad_down = None
    for n, part in enumerate(parts):
        pre = pres[n]
        square = pre * pre
        inner = jnp.tanh(pre * (GELU_C + (GELU_C * 0.044715) * square))
        half = 0.5 + 0.5 * inner
        hidden = (pre * half).astype(jnp.bfloat16)
        slope = half + (0.5 * pre) * (1.0 - inner * inner) * (
            GELU_C + (3.0 * 0.044715 * GELU_C) * square
        )
        pre_grad = (backs[n] * slope).astype(jnp.bfloat16)
        hid_ref[:, part] = hidden
        pg_ref[:, part] = pre_grad
        by_up = nn(pre_grad, x_ref[part])
        by_down = nn(hidden, g_ref[part])
        grad_up = by_up if grad_up is None else grad_up + by_up
        grad_down = by_down if grad_down is None else grad_down + by_down
    grads_ref[:, :width] = grad_up.astype(jnp.bfloat16).reshape(shards, width, feature)
    grads_ref[:, width:] = grad_down.astype(jnp.bfloat16).reshape(shards, width, feature)


def middle(weights, slot_x, slot_g):
    owners, _, width, feature = weights.shape
    rows = slot_x.shape[0]
    step = owners // CHUNKS
    ff = owners * width
    return pl.pallas_call(
        middle_kernel,
        grid=(CHUNKS,),
        in_specs=[
            pl.BlockSpec((step, 2, width, feature), lambda i: (i, 0, 0, 0)),
            pl.BlockSpec((rows, feature), lambda i: (0, 0)),
            pl.BlockSpec((rows, feature), lambda i: (0, 0)),
        ],
        out_specs=[
            pl.BlockSpec((step, 2 * width, feature), lambda i: (i, 0, 0)),
            pl.BlockSpec((step * width, rows), lambda i: (i, 0)),
            pl.BlockSpec((step * width, rows), lambda i: (i, 0)),
        ],
        out_shape=[
            pltpu.HBM((owners, 2 * width, feature), jnp.bfloat16),
            pltpu.HBM((ff, rows), jnp.bfloat16),
            pltpu.HBM((ff, rows), jnp.bfloat16),
        ],
        compiler_params=pltpu.CompilerParams(vmem_limit_bytes=MIDDLE_LIMIT),
        cost_estimate=pl.CostEstimate(
            flops=8 * rows * ff * feature,
            bytes_accessed=8 * ff * feature + 4 * ff * rows,
            transcendentals=ff * rows,
        ),
        name="middle",
    )(weights, slot_x, slot_g)


def back_kernel(side, w_ref, act_ref, out_ref, acc):
    shards, _, width, feature = w_ref.shape
    matrix = w_ref[:, 0].reshape(shards * width, feature)

    @pl.when(pl.program_id(0) == 0)
    def _():
        acc[...] = jnp.zeros_like(acc)

    acc[...] += tn(act_ref[...], matrix)

    @pl.when(pl.program_id(0) == pl.num_programs(0) - 1)
    def _():
        out_ref[...] = acc[...].astype(jnp.bfloat16)


def back(weights, activity, side):
    owners, _, width, feature = weights.shape
    ff, rows = activity.shape
    steps = 2
    step = owners // steps
    return pl.pallas_call(
        functools.partial(back_kernel, side),
        grid=(steps,),
        in_specs=[
            pl.BlockSpec((step, 1, width, feature), lambda i: (i, side, 0, 0)),
            pl.BlockSpec((step * width, rows), lambda i: (i, 0)),
        ],
        out_specs=pl.BlockSpec((rows, feature), lambda i: (0, 0)),
        out_shape=jax.ShapeDtypeStruct((rows, feature), jnp.bfloat16),
        scratch_shapes=[pltpu.VMEM((rows, feature), jnp.float32)],
        compiler_params=pltpu.CompilerParams(vmem_limit_bytes=VMEM_LIMIT),
        cost_estimate=pl.CostEstimate(
            flops=2 * rows * ff * feature,
            bytes_accessed=2 * ff * feature + 2 * ff * rows,
            transcendentals=0,
        ),
        name="back",
    )(weights, activity)


def window_index(row, col, tile):
    wins = (tile + 2 * margin_cells) // window_side
    window = (row // window_side) * wins + col // window_side
    return (window * window_side + row % window_side) * window_side + col % window_side


def tile_top(tile, odd, other):
    return margin_cells + tile * ((1 - odd) if other else odd)


def edge_top(tile, odd, far):
    high = (1 - odd) if far else odd
    return (2 * tile + margin_cells) * high


def into_windows(tile, odd):
    margin, base = margin_cells, tile * tile
    tall = 2 * tile + 2 * margin
    edge, strip = margin * tile, margin * tall
    cells = tall * (tile + 2 * margin)
    piece = lax.broadcasted_iota(jnp.int32, (1, cells), 1)
    in_tile = piece % base
    row = tile_top(tile, odd, False) + in_tile // tile
    row = jnp.where(piece >= base, tile_top(tile, odd, True) + in_tile // tile, row)
    col = margin + in_tile % tile
    start = 2 * base
    for far in (False, True):
        row = jnp.where(piece >= start, edge_top(tile, odd, far) + (piece - start) // tile, row)
        start += edge
    for side in (0, margin + tile):
        at = (piece - start) // margin
        side_row = edge_top(tile, odd, False) + at
        side_row = jnp.where(at >= margin, tile_top(tile, odd, False) + at - margin, side_row)
        side_row = jnp.where(
            at >= margin + tile, tile_top(tile, odd, True) + at - margin - tile, side_row
        )
        side_row = jnp.where(
            at >= margin + 2 * tile, edge_top(tile, odd, True) + at - margin - 2 * tile, side_row
        )
        row = jnp.where(piece >= start, side_row, row)
        col = jnp.where(piece >= start, side + (piece - start) % margin, col)
        start += strip
    place = window_index(row, col, tile)
    return one_hot(lax.broadcasted_iota(jnp.int32, (cells, cells), 0) == place)


def out_of_windows(tile, odd):
    base = tile * tile
    cells = (2 * tile + 2 * margin_cells) * (tile + 2 * margin_cells)
    token = lax.broadcasted_iota(jnp.int32, (2 * base, 1), 0)
    in_tile = token % base
    top = jnp.where(token >= base, tile_top(tile, odd, True), tile_top(tile, odd, False))
    place = window_index(top + in_tile // tile, margin_cells + in_tile % tile, tile)
    return one_hot(lax.broadcasted_iota(jnp.int32, (2 * base, cells), 1) == place)


def front_kernel(
    at_ref, target_ref, own_ref, other_ref, near_ref, far_ref, left_ref, right_ref, wqkv_ref, wproj_ref,
    mixed_ref, slots_ref, qkv_ref, ctx_ref,
):
    bf16, f32 = jnp.bfloat16, jnp.float32
    count, feature = own_ref.shape
    tile = math.isqrt(count)
    cells = window_side * window_side
    head = feature // HEADS
    group = 128 // head
    odd = at_ref[0] % 2
    tokens = jnp.concatenate([own_ref[...], other_ref[...]], axis=0)
    pieces = jnp.concatenate(
        [tokens, near_ref[...], far_ref[...], left_ref[...], right_ref[...]], axis=0
    )
    placed = nn(into_windows(tile, odd), pieces).astype(bf16)
    for part in range(3):
        columns = slice(part * feature, (part + 1) * feature)
        qkv_ref[:, columns] = nn(placed, wqkv_ref[:, columns]).astype(bf16)
    first_row, last_row = at_ref[0] < 2, at_ref[0] >= at_ref[1] - 2
    first_col, last_col = at_ref[2] == 0, at_ref[2] == at_ref[3] - 1
    lane = lax.broadcasted_iota(jnp.int32, (1, 128), 1)
    own = [
        ((lane >= h * head) & (lane < (h + 1) * head)).astype(f32) for h in range(group)
    ]
    own16 = [o.astype(bf16) for o in own]
    key = lax.broadcasted_iota(jnp.int32, (cells, 128), 0)
    key_row, key_col = key // window_side, key % window_side
    half = window_side // 2
    low_bias = jnp.float32(-1e30)
    edge_bias = {
        (0, 0): jnp.where(key_row < half, jnp.where(first_row, low_bias, 0.0), 0.0),
        (0, 4): jnp.where(key_row >= half, jnp.where(last_row, low_bias, 0.0), 0.0),
        (1, 0): jnp.where(key_col < half, jnp.where(first_col, low_bias, 0.0), 0.0),
        (1, 2): jnp.where(key_col >= half, jnp.where(last_col, low_bias, 0.0), 0.0),
    }
    scale = 1.0 / math.sqrt(head)
    for window in range(15):
        wi, wj = window // 3, window % 3
        bias = None
        if wi in (0, 4):
            bias = edge_bias[0, wi]
        if wj != 1:
            bias = edge_bias[1, wj] if bias is None else bias + edge_bias[1, wj]
        if bias is not None:
            bias = jnp.concatenate([bias] * (group * cells // 128), axis=1)
        rows = slice(window * cells, (window + 1) * cells)
        for g in range(feature // 128):
            q = qkv_ref[rows, g * 128 : (g + 1) * 128]
            k = qkv_ref[rows, feature + g * 128 : feature + (g + 1) * 128]
            v = qkv_ref[rows, 2 * feature + g * 128 : 2 * feature + (g + 1) * 128]
            spread = jnp.concatenate([q * o for o in own16], axis=0)
            scores = nt(k, spread)
            if bias is not None:
                scores = scores + bias
            peak = jnp.max(scores, axis=0, keepdims=True)
            weights = jnp.exp((scores - peak) * scale)
            probs = (weights * (1.0 / jnp.sum(weights, axis=0, keepdims=True))).astype(bf16)
            wide = tn(probs, v)
            mine = wide[:cells] * own[0]
            for h in range(1, group):
                mine = mine + wide[h * cells : (h + 1) * cells] * own[h]
            ctx_ref[rows, g * 128 : (g + 1) * 128] = mine.astype(bf16)
    context = nn(out_of_windows(tile, odd), ctx_ref[...]).astype(bf16)
    attended = nn(context, wproj_ref[...])
    centred = attended - jnp.mean(attended, axis=-1, keepdims=True)
    spread_of = jnp.mean(centred * centred, axis=-1, keepdims=True)
    mixed = (tokens.astype(f32) + centred * lax.rsqrt(spread_of + 1e-05)).astype(bf16)
    mixed_ref[...] = mixed[:count]
    rows = slots_ref.shape[0]
    slots = nn(placer(target_ref[0:1], rows), mixed[:count])
    slots = slots + nn(placer(target_ref[1:2], rows), mixed[count:])
    slots_ref[...] = slots.astype(bf16)


def front(at, target, own, other, near, far, left, right, w_qkv, w_proj, slot_count):
    count, feature = own.shape
    tile = math.isqrt(count)
    cells = (2 * tile + 2 * margin_cells) * (tile + 2 * margin_cells)
    smem = pl.BlockSpec(memory_space=pltpu.SMEM)
    vmem = pl.BlockSpec(memory_space=pltpu.VMEM)
    return vmem_call(
        front_kernel,
        [((count, feature), jnp.bfloat16), ((slot_count, feature), jnp.bfloat16)],
        "front",
        7_000_000_000,
        in_specs=[smem] + [vmem] * 9,
        scratch_shapes=[
            pltpu.VMEM((cells, 3 * feature), jnp.bfloat16),
            pltpu.VMEM((cells, feature), jnp.bfloat16),
        ],
    )(at, target, own, other, near, far, left, right, w_qkv, w_proj)


def shifts(axis):
    count = lax.axis_size(axis)
    forward = [(i, i + 1) for i in range(count - 1)]
    return forward, [(target, source) for source, target in forward]


def sharing(axis):
    count = lax.axis_size(axis)
    groups = [list(range(parity, count, 2)) for parity in range(2)]
    return groups, [(i, i ^ 1) for i in range(count)]


def pair_edges(axis):
    count = lax.axis_size(axis)
    near = [(z, z + 1) for z in range(1, count - 1, 2)]
    near += [(z, z - 1) for z in range(2, count, 2)]
    far = [(z, z + 2) for z in range(1, count - 2, 2)]
    far += [(z, z - 2) for z in range(2, count, 2)]
    return near, far


def per_device(tokens, gate, route, cotangent, w_qkv, w_proj, w_up, w_down):
    tile_rows, tile_cols, feature = tokens.shape
    tok_count = tile_rows * tile_cols
    margin = margin_cells
    experts = lax.axis_size("exp")
    capacity = max(2, 3 * tok_count // (2 * experts))
    slot_count = 2 * experts * capacity
    bf16, f32 = jnp.bfloat16, jnp.float32
    rows_of = ((slot_count, feature), bf16)
    groups, swap = sharing("rep")

    def dispatch(rows):
        blocks = rows.reshape(experts, -1, feature)
        return lax.all_to_all(blocks, "exp", 0, 0, tiled=True).reshape(-1, feature)

    weights = lax.all_gather(
        jnp.concatenate([w_up, w_down], axis=0),
        "rep",
        axis=0,
        tiled=False,
        axis_index_groups=groups,
    )
    near_swap, far_swap = pair_edges("rep")
    odd = lax.axis_index("rep") % 2
    edge = jnp.where(odd == 0, tokens[:margin], tokens[tile_rows - margin :])
    other = lax.ppermute(tokens, "rep", swap)
    near = lax.ppermute(edge, "rep", near_swap)
    far = lax.ppermute(edge, "rep", far_swap)
    gate_rows = gate.reshape(tok_count, 1)
    [give] = vmem_call(
        upstream_kernel, [((tok_count + EXTRA, feature), bf16)], "upstream", 1_000_000, count=3
    )(route.reshape(1, tok_count), gate_rows, cotangent.reshape(tok_count, feature))
    got = lax.ppermute(give, "rep", swap)
    forward, backward = shifts("exp")

    def strip(cols):
        parts = [near[:, cols], tokens[:, cols], other[:, cols], far[:, cols]]
        return jnp.concatenate(parts, axis=0).reshape(-1, feature)

    left = lax.ppermute(strip(slice(tile_cols - margin, tile_cols)), "exp", forward)
    right = lax.ppermute(strip(slice(0, margin)), "exp", backward)
    at = jnp.stack(
        [
            lax.axis_index("rep"),
            jnp.int32(lax.axis_size("rep")),
            lax.axis_index("exp"),
            jnp.int32(experts),
        ]
    ).astype(jnp.int32)
    slots_g, target = vmem_call(
        functools.partial(grad_slots_kernel, experts, capacity),
        [rows_of, ((2, tok_count), jnp.int32)],
        "grad_slots",
        500_000_000,
        count=2,
    )(give, got)
    slot_g = dispatch(slots_g)
    mixed, slots_x = front(
        at,
        target,
        tokens.reshape(tok_count, feature),
        other.reshape(tok_count, feature),
        near.reshape(-1, feature),
        far.reshape(-1, feature),
        left,
        right,
        w_qkv,
        w_proj,
        slot_count,
    )
    slot_x = dispatch(slots_x)
    grads, hidden, pre_grad = middle(weights, slot_x, slot_g)
    summed = lax.psum_scatter(
        grads, "rep", scatter_dimension=0, tiled=True, axis_index_groups=groups
    )

    def exchanged(rows):
        [theirs] = vmem_call(
            back_rows_kernel, [((tok_count, feature), bf16)], "back_rows", 200_000_000, count=2
        )(target, rows)
        return lax.ppermute(theirs, "rep", swap)

    back_out = dispatch(back(weights, hidden, 1))
    back_in = dispatch(back(weights, pre_grad, 0))
    got_out = exchanged(back_out)
    back_in, got_out = lax.optimization_barrier((back_in, got_out))
    layer_out, input_grad = vmem_call(
        combine_kernel, [((tok_count, feature), bf16)] * 2, "combine", 400_000_000, count=7
    )(target, back_out, got_out, back_in, exchanged(back_in), mixed, gate_rows)
    grad_up, grad_down = vmem_call(
        functools.partial(gradients_kernel, 1.0 / lax.axis_size("rep")),
        [(w_up.shape, f32)] * 2,
        "gradients",
        1_000_000,
        count=1,
    )(summed)
    return (
        layer_out.reshape(tile_rows, tile_cols, feature),
        input_grad.reshape(tile_rows, tile_cols, feature),
        grad_up,
        grad_down,
    )


def solution(mesh):
    placed = (
        P("rep", "exp", None),
        P("rep", "exp"),
        P("rep", "exp", None, None),
        P("rep", "exp", None),
        P(),
        P(),
        P("exp", "rep", None),
        P("exp", "rep", None),
    )
    return jax.shard_map(
        per_device,
        mesh=mesh,
        in_specs=placed,
        out_specs=(
            P("rep", "exp", None),
            P("rep", "exp", None),
            P("exp", "rep", None),
            P("exp", "rep", None),
        ),
        check_vma=False,
    )
```

```python
import functools
import math

import jax
import jax.numpy as jnp
from jax import lax
from jax.experimental import pallas as pl
from jax.experimental.pallas import tpu as pltpu
from jax.sharding import PartitionSpec as P

HEADS = 16


GELU_C = math.sqrt(2.0 / math.pi)
window_side = 8
margin_cells = 4
CHUNKS = 4
EXTRA = 16

VMEM_LIMIT = 24 * 1024 * 1024
MIDDLE_LIMIT = 58 * 1024 * 1024


def nt(a, b):
    return lax.dot_general(a, b, (((1,), (1,)), ((), ())), preferred_element_type=jnp.float32)


def tn(a, b):
    return lax.dot_general(a, b, (((0,), (0,)), ((), ())), preferred_element_type=jnp.float32)


def nn(a, b):
    return jnp.dot(a, b, preferred_element_type=jnp.float32)


def one_hot(mask):
    return mask.astype(jnp.float32).astype(jnp.bfloat16)


def vmem_call(kernel, out, name, flops, in_specs=None, count=0, **more):
    vmem = pl.BlockSpec(memory_space=pltpu.VMEM)
    return pl.pallas_call(
        kernel,
        in_specs=in_specs or [vmem] * count,
        out_specs=[vmem] * len(out),
        out_shape=[jax.ShapeDtypeStruct(shape, dtype) for shape, dtype in out],
        compiler_params=pltpu.CompilerParams(vmem_limit_bytes=VMEM_LIMIT),
        cost_estimate=pl.CostEstimate(flops=flops, bytes_accessed=3_000_000, transcendentals=0),
        name=name,
        **more,
    )


def upstream_kernel(route_ref, gate_ref, cot_ref, give_ref):
    f32, bf16 = jnp.float32, jnp.bfloat16
    count, feature = cot_ref.shape
    give_ref[:count] = (gate_ref[...] * cot_ref[...].astype(f32)).astype(bf16)
    route = route_ref[...].astype(f32)
    row = jnp.concatenate([route, jnp.zeros((1, feature - count), f32)], axis=1)
    extra = give_ref.shape[0] - count
    give_ref[count:] = jnp.broadcast_to(row, (extra, feature)).astype(bf16)


def slot_numbers(route, experts):
    count = route.shape[1]
    matches = lax.broadcasted_iota(jnp.int32, (experts, count), 0) == route
    earlier = lax.broadcasted_iota(jnp.int32, (count, count), 0) < lax.broadcasted_iota(
        jnp.int32, (count, count), 1
    )
    before = nn(one_hot(matches), one_hot(earlier))
    return jnp.sum(jnp.where(matches, before, 0.0), axis=0, keepdims=True).astype(jnp.int32)


def placer(target, rows):
    return one_hot(lax.broadcasted_iota(jnp.int32, (rows, target.shape[1]), 0) == target)


def grad_slots_kernel(experts, capacity, give_ref, got_ref, slots_ref, target_ref):
    feature = give_ref.shape[1]
    count = give_ref.shape[0] - EXTRA
    total = None
    for n, ref in enumerate((give_ref, got_ref)):
        route = ref[count:, :count].astype(jnp.float32)[:1].astype(jnp.int32)
        target = route * (2 * capacity) + n * capacity + slot_numbers(route, experts)
        target_ref[n : n + 1] = target
        placed = nn(placer(target, 2 * experts * capacity), ref[:count])
        total = placed if total is None else total + placed
    slots_ref[...] = total.astype(jnp.bfloat16)


def token_slots_kernel(target_ref, mixed_ref, got_ref, slots_ref):
    rows = slots_ref.shape[0]
    total = nn(placer(target_ref[0:1], rows), mixed_ref[...])
    total = total + nn(placer(target_ref[1:2], rows), got_ref[...])
    slots_ref[...] = total.astype(jnp.bfloat16)


def back_rows_kernel(target_ref, back_ref, give_ref):
    give_ref[...] = tn(placer(target_ref[1:2], back_ref.shape[0]), back_ref[...]).astype(
        jnp.bfloat16
    )


def combine_kernel(
    target_ref, out_ref, got_out_ref, in_ref, got_in_ref, mixed_ref, gate_ref, layer_ref, grad_ref
):
    f32, bf16 = jnp.float32, jnp.bfloat16
    mine = placer(target_ref[0:1], out_ref.shape[0])
    token_out = tn(mine, out_ref[...]) + got_out_ref[...].astype(f32)
    layer_ref[...] = (mixed_ref[...].astype(f32) + gate_ref[...] * token_out).astype(bf16)
    grad_ref[...] = (tn(mine, in_ref[...]) + got_in_ref[...].astype(f32)).astype(bf16)


def gradients_kernel(scale, sum_ref, up_ref, down_ref):
    width = up_ref.shape[1]
    up_ref[0] = sum_ref[0, :width].astype(jnp.float32) * scale
    down_ref[0] = sum_ref[0, width:].astype(jnp.float32) * scale


def middle_kernel(w_ref, x_ref, g_ref, grads_ref, hid_ref, pg_ref):
    shards, _, width, feature = w_ref.shape
    up = w_ref[:, 0].reshape(shards * width, feature)
    down = w_ref[:, 1].reshape(shards * width, feature)
    halves = 2
    rows = x_ref.shape[0] // halves
    parts = [slice(n * rows, (n + 1) * rows) for n in range(halves)]
    pres = [nt(up, x_ref[part]) for part in parts]
    backs = [nt(down, g_ref[part]) for part in parts]
    grad_up = grad_down = None
    for n, part in enumerate(parts):
        pre = pres[n]
        square = pre * pre
        inner = jnp.tanh(pre * (GELU_C + (GELU_C * 0.044715) * square))
        half = 0.5 + 0.5 * inner
        hidden = (pre * half).astype(jnp.bfloat16)
        slope = half + (0.5 * pre) * (1.0 - inner * inner) * (
            GELU_C + (3.0 * 0.044715 * GELU_C) * square
        )
        pre_grad = (backs[n] * slope).astype(jnp.bfloat16)
        hid_ref[:, part] = hidden
        pg_ref[:, part] = pre_grad
        by_up = nn(pre_grad, x_ref[part])
        by_down = nn(hidden, g_ref[part])
        grad_up = by_up if grad_up is None else grad_up + by_up
        grad_down = by_down if grad_down is None else grad_down + by_down
    grads_ref[:, :width] = grad_up.astype(jnp.bfloat16).reshape(shards, width, feature)
    grads_ref[:, width:] = grad_down.astype(jnp.bfloat16).reshape(shards, width, feature)


def middle(weights, slot_x, slot_g):
    owners, _, width, feature = weights.shape
    rows = slot_x.shape[0]
    step = owners // CHUNKS
    ff = owners * width
    return pl.pallas_call(
        middle_kernel,
        grid=(CHUNKS,),
        in_specs=[
            pl.BlockSpec((step, 2, width, feature), lambda i: (i, 0, 0, 0)),
            pl.BlockSpec((rows, feature), lambda i: (0, 0)),
            pl.BlockSpec((rows, feature), lambda i: (0, 0)),
        ],
        out_specs=[
            pl.BlockSpec((step, 2 * width, feature), lambda i: (i, 0, 0)),
            pl.BlockSpec((step * width, rows), lambda i: (i, 0)),
            pl.BlockSpec((step * width, rows), lambda i: (i, 0)),
        ],
        out_shape=[
            pltpu.HBM((owners, 2 * width, feature), jnp.bfloat16),
            pltpu.HBM((ff, rows), jnp.bfloat16),
            pltpu.HBM((ff, rows), jnp.bfloat16),
        ],
        compiler_params=pltpu.CompilerParams(vmem_limit_bytes=MIDDLE_LIMIT),
        cost_estimate=pl.CostEstimate(
            flops=8 * rows * ff * feature,
            bytes_accessed=8 * ff * feature + 4 * ff * rows,
            transcendentals=ff * rows,
        ),
        name="middle",
    )(weights, slot_x, slot_g)


def back_kernel(side, w_ref, act_ref, out_ref, acc):
    shards, _, width, feature = w_ref.shape
    matrix = w_ref[:, 0].reshape(shards * width, feature)

    @pl.when(pl.program_id(0) == 0)
    def _():
        acc[...] = jnp.zeros_like(acc)

    acc[...] += tn(act_ref[...], matrix)

    @pl.when(pl.program_id(0) == pl.num_programs(0) - 1)
    def _():
        out_ref[...] = acc[...].astype(jnp.bfloat16)


def back(weights, activity, side):
    owners, _, width, feature = weights.shape
    ff, rows = activity.shape
    steps = 2
    step = owners // steps
    return pl.pallas_call(
        functools.partial(back_kernel, side),
        grid=(steps,),
        in_specs=[
            pl.BlockSpec((step, 1, width, feature), lambda i: (i, side, 0, 0)),
            pl.BlockSpec((step * width, rows), lambda i: (i, 0)),
        ],
        out_specs=pl.BlockSpec((rows, feature), lambda i: (0, 0)),
        out_shape=jax.ShapeDtypeStruct((rows, feature), jnp.bfloat16),
        scratch_shapes=[pltpu.VMEM((rows, feature), jnp.float32)],
        compiler_params=pltpu.CompilerParams(vmem_limit_bytes=VMEM_LIMIT),
        cost_estimate=pl.CostEstimate(
            flops=2 * rows * ff * feature,
            bytes_accessed=2 * ff * feature + 2 * ff * rows,
            transcendentals=0,
        ),
        name="back",
    )(weights, activity)


def window_index(row, col, tile):
    wins = (tile + 2 * margin_cells) // window_side
    window = (row // window_side) * wins + col // window_side
    return (window * window_side + row % window_side) * window_side + col % window_side


def into_windows(tile):
    ext = tile + 2 * margin_cells
    edge, strip = margin_cells * tile, margin_cells * ext
    piece = lax.broadcasted_iota(jnp.int32, (1, ext * ext), 1)
    base = tile * tile
    row, col = margin_cells + piece // tile, margin_cells + piece % tile
    low = piece - base
    row = jnp.where(piece >= base, low // tile, row)
    high = piece - (base + edge)
    row = jnp.where(piece >= base + edge, tile + margin_cells + high // tile, row)
    left = piece - (base + 2 * edge)
    side = piece >= base + 2 * edge
    row = jnp.where(side, left // margin_cells, row)
    col = jnp.where(side, left % margin_cells, col)
    right = left - strip
    side = piece >= base + 2 * edge + strip
    row = jnp.where(side, right // margin_cells, row)
    col = jnp.where(side, tile + margin_cells + right % margin_cells, col)
    place = window_index(row, col, tile)
    return one_hot(lax.broadcasted_iota(jnp.int32, (ext * ext, ext * ext), 0) == place)


def out_of_windows(tile):
    ext = tile + 2 * margin_cells
    token = lax.broadcasted_iota(jnp.int32, (tile * tile, 1), 0)
    place = window_index(token // tile + margin_cells, token % tile + margin_cells, tile)
    return one_hot(lax.broadcasted_iota(jnp.int32, (tile * tile, ext * ext), 1) == place)


def front_kernel(
    at_ref, tok_ref, low_ref, high_ref, left_ref, right_ref, wqkv_ref, wproj_ref, mixed_ref, qkv_ref, ctx_ref
):
    bf16, f32 = jnp.bfloat16, jnp.float32
    tokens = tok_ref[...]
    count, feature = tokens.shape
    cells = window_side * window_side
    head = feature // HEADS
    group = 128 // head
    pieces = jnp.concatenate(
        [tokens, low_ref[...], high_ref[...], left_ref[...], right_ref[...]], axis=0
    )
    placed = nn(into_windows(math.isqrt(count)), pieces).astype(bf16)
    qkv_ref[...] = jnp.dot(placed, wqkv_ref[...], preferred_element_type=f32).astype(bf16)
    first_row, last_row = at_ref[0] == 0, at_ref[0] == at_ref[1] - 1
    first_col, last_col = at_ref[2] == 0, at_ref[2] == at_ref[3] - 1
    lane = lax.broadcasted_iota(jnp.int32, (1, 128), 1)
    own = [
        ((lane >= h * head) & (lane < (h + 1) * head)).astype(f32) for h in range(group)
    ]
    own16 = [o.astype(bf16) for o in own]
    key = lax.broadcasted_iota(jnp.int32, (cells, 128), 0)
    key_row, key_col = key // window_side, key % window_side
    half = window_side // 2
    low_bias = jnp.float32(-1e30)
    edge_bias = {
        (0, 0): jnp.where(key_row < half, jnp.where(first_row, low_bias, 0.0), 0.0),
        (0, 2): jnp.where(key_row >= half, jnp.where(last_row, low_bias, 0.0), 0.0),
        (1, 0): jnp.where(key_col < half, jnp.where(first_col, low_bias, 0.0), 0.0),
        (1, 2): jnp.where(key_col >= half, jnp.where(last_col, low_bias, 0.0), 0.0),
    }
    scale = 1.0 / math.sqrt(head)
    for window in range(9):
        wi, wj = window // 3, window % 3
        bias = None
        if wi != 1:
            bias = edge_bias[0, wi]
        if wj != 1:
            bias = edge_bias[1, wj] if bias is None else bias + edge_bias[1, wj]
        if bias is not None:
            bias = jnp.concatenate([bias] * (group * cells // 128), axis=1)
        rows = slice(window * cells, (window + 1) * cells)
        for g in range(feature // 128):
            q = qkv_ref[rows, g * 128 : (g + 1) * 128]
            k = qkv_ref[rows, feature + g * 128 : feature + (g + 1) * 128]
            v = qkv_ref[rows, 2 * feature + g * 128 : 2 * feature + (g + 1) * 128]
            spread = jnp.concatenate([q * o for o in own16], axis=0)
            scores = nt(k, spread)
            if bias is not None:
                scores = scores + bias
            peak = jnp.max(scores, axis=0, keepdims=True)
            weights = jnp.exp((scores - peak) * scale)
            probs = (weights * (1.0 / jnp.sum(weights, axis=0, keepdims=True))).astype(bf16)
            wide = tn(probs, v)
            mine = wide[:cells] * own[0]
            for h in range(1, group):
                mine = mine + wide[h * cells : (h + 1) * cells] * own[h]
            ctx_ref[rows, g * 128 : (g + 1) * 128] = mine.astype(bf16)
    context = nn(out_of_windows(math.isqrt(count)), ctx_ref[...]).astype(bf16)
    attended = jnp.dot(context, wproj_ref[...], preferred_element_type=f32)
    centred = attended - jnp.mean(attended, axis=-1, keepdims=True)
    spread_of = jnp.mean(centred * centred, axis=-1, keepdims=True)
    mixed = (tokens.astype(f32) + centred * lax.rsqrt(spread_of + 1e-05)).astype(bf16)
    mixed_ref[...] = mixed


def front(at, tokens, low, high, left, right, w_qkv, w_proj):
    count, feature = tokens.shape
    ext = (math.isqrt(count) + 2 * margin_cells) ** 2
    smem = pl.BlockSpec(memory_space=pltpu.SMEM)
    vmem = pl.BlockSpec(memory_space=pltpu.VMEM)
    return vmem_call(
        front_kernel,
        [((count, feature), jnp.bfloat16)],
        "front",
        4_000_000_000,
        in_specs=[smem] + [vmem] * 7,
        scratch_shapes=[
            pltpu.VMEM((ext, 3 * feature), jnp.bfloat16),
            pltpu.VMEM((ext, feature), jnp.bfloat16),
        ],
    )(at, tokens, low, high, left, right, w_qkv, w_proj)[0]


def shifts(axis):
    count = lax.axis_size(axis)
    forward = [(i, i + 1) for i in range(count - 1)]
    return forward, [(target, source) for source, target in forward]


def sharing():
    count, width = lax.axis_size("rep"), lax.axis_size("exp")
    groups = [list(range(parity, count, 2)) for parity in range(2)]
    swap = []
    for rep in range(count):
        for exp in range(width):
            partner = (rep + 1) % count if (rep + exp) % 2 == 0 else (rep - 1) % count
            swap.append((rep * width + exp, partner * width + exp))
    return groups, swap


def per_device(tokens, gate, route, cotangent, w_qkv, w_proj, w_up, w_down):
    tile_rows, tile_cols, feature = tokens.shape
    tok_count = tile_rows * tile_cols
    margin = margin_cells
    experts = lax.axis_size("exp")
    capacity = max(2, 3 * tok_count // (2 * experts))
    slot_count = 2 * experts * capacity
    bf16, f32 = jnp.bfloat16, jnp.float32
    rows_of = ((slot_count, feature), bf16)
    groups, swap = sharing()

    def exchange(rows):
        return lax.ppermute(rows, ("rep", "exp"), swap)

    def dispatch(rows):
        blocks = rows.reshape(experts, -1, feature)
        return lax.all_to_all(blocks, "exp", 0, 0, tiled=True).reshape(-1, feature)

    weights = lax.all_gather(
        jnp.concatenate([w_up, w_down], axis=0),
        "rep",
        axis=0,
        tiled=False,
        axis_index_groups=groups,
    )
    forward, backward = shifts("rep")
    low = lax.ppermute(tokens[tile_rows - margin :], "rep", forward)
    high = lax.ppermute(tokens[:margin], "rep", backward)
    gate_rows = gate.reshape(tok_count, 1)
    [give] = vmem_call(
        upstream_kernel, [((tok_count + EXTRA, feature), bf16)], "upstream", 1_000_000, count=3
    )(route.reshape(1, tok_count), gate_rows, cotangent.reshape(tok_count, feature))
    got = exchange(give)
    forward, backward = shifts("exp")

    def strip(cols):
        parts = [low[:, cols], tokens[:, cols], high[:, cols]]
        return jnp.concatenate(parts, axis=0).reshape(-1, feature)

    left = lax.ppermute(strip(slice(tile_cols - margin, tile_cols)), "exp", forward)
    right = lax.ppermute(strip(slice(0, margin)), "exp", backward)
    at = jnp.stack(
        [
            lax.axis_index("rep"),
            jnp.int32(lax.axis_size("rep")),
            lax.axis_index("exp"),
            jnp.int32(experts),
        ]
    ).astype(jnp.int32)
    mixed = front(
        at,
        tokens.reshape(tok_count, feature),
        low.reshape(-1, feature),
        high.reshape(-1, feature),
        left,
        right,
        w_qkv,
        w_proj,
    )
    got_mixed = exchange(mixed)
    slots_g, target = vmem_call(
        functools.partial(grad_slots_kernel, experts, capacity),
        [rows_of, ((2, tok_count), jnp.int32)],
        "grad_slots",
        500_000_000,
        count=2,
    )(give, got)
    slot_g = dispatch(slots_g)
    [slots_x] = vmem_call(token_slots_kernel, [rows_of], "token_slots", 400_000_000, count=3)(
        target, mixed, got_mixed
    )
    slot_x = dispatch(slots_x)
    grads, hidden, pre_grad = middle(weights, slot_x, slot_g)
    summed = lax.psum_scatter(
        grads, "rep", scatter_dimension=0, tiled=True, axis_index_groups=groups
    )

    def exchanged(rows):
        [theirs] = vmem_call(
            back_rows_kernel, [((tok_count, feature), bf16)], "back_rows", 200_000_000, count=2
        )(target, rows)
        return exchange(theirs)

    back_out = dispatch(back(weights, hidden, 1))
    back_in = dispatch(back(weights, pre_grad, 0))
    got_out = exchanged(back_out)
    back_in, got_out = lax.optimization_barrier((back_in, got_out))
    layer_out, input_grad = vmem_call(
        combine_kernel, [((tok_count, feature), bf16)] * 2, "combine", 400_000_000, count=7
    )(target, back_out, got_out, back_in, exchanged(back_in), mixed, gate_rows)
    grad_up, grad_down = vmem_call(
        functools.partial(gradients_kernel, 1.0 / lax.axis_size("rep")),
        [(w_up.shape, f32)] * 2,
        "gradients",
        1_000_000,
        count=1,
    )(summed)
    return (
        layer_out.reshape(tile_rows, tile_cols, feature),
        input_grad.reshape(tile_rows, tile_cols, feature),
        grad_up,
        grad_down,
    )


def solution(mesh):
    placed = (
        P("rep", "exp", None),
        P("rep", "exp"),
        P("rep", "exp", None, None),
        P("rep", "exp", None),
        P(),
        P(),
        P("exp", "rep", None),
        P("exp", "rep", None),
    )
    return jax.shard_map(
        per_device,
        mesh=mesh,
        in_specs=placed,
        out_specs=(
            P("rep", "exp", None),
            P("rep", "exp", None),
            P("exp", "rep", None),
            P("exp", "rep", None),
        ),
        check_vma=False,
    )
```

```python
import functools
import math

import jax
import jax.numpy as jnp
from jax import lax
from jax.experimental import pallas as pl
from jax.experimental.pallas import tpu as pltpu
from jax.sharding import PartitionSpec as P

HEADS = 16


GELU_C = math.sqrt(2.0 / math.pi)
window_side = 8
margin_cells = 4
CHUNKS = 4
EXTRA = 16

VMEM_LIMIT = 24 * 1024 * 1024
MIDDLE_LIMIT = 58 * 1024 * 1024


def nt(a, b):
    return lax.dot_general(a, b, (((1,), (1,)), ((), ())), preferred_element_type=jnp.float32)


def tn(a, b):
    return lax.dot_general(a, b, (((0,), (0,)), ((), ())), preferred_element_type=jnp.float32)


def nn(a, b):
    return jnp.dot(a, b, preferred_element_type=jnp.float32)


def one_hot(mask):
    return mask.astype(jnp.float32).astype(jnp.bfloat16)


def vmem_call(kernel, out, name, flops, in_specs=None, count=0, **more):
    vmem = pl.BlockSpec(memory_space=pltpu.VMEM)
    return pl.pallas_call(
        kernel,
        in_specs=in_specs or [vmem] * count,
        out_specs=[vmem] * len(out),
        out_shape=[jax.ShapeDtypeStruct(shape, dtype) for shape, dtype in out],
        compiler_params=pltpu.CompilerParams(vmem_limit_bytes=VMEM_LIMIT),
        cost_estimate=pl.CostEstimate(flops=flops, bytes_accessed=3_000_000, transcendentals=0),
        name=name,
        **more,
    )


def upstream_kernel(route_ref, gate_ref, cot_ref, give_ref):
    f32, bf16 = jnp.float32, jnp.bfloat16
    count, feature = cot_ref.shape
    give_ref[:count] = (gate_ref[...] * cot_ref[...].astype(f32)).astype(bf16)
    route = route_ref[...].astype(f32)
    row = jnp.concatenate([route, jnp.zeros((1, feature - count), f32)], axis=1)
    extra = give_ref.shape[0] - count
    give_ref[count:] = jnp.broadcast_to(row, (extra, feature)).astype(bf16)


def slot_numbers(route, experts):
    count = route.shape[1]
    matches = lax.broadcasted_iota(jnp.int32, (experts, count), 0) == route
    earlier = lax.broadcasted_iota(jnp.int32, (count, count), 0) < lax.broadcasted_iota(
        jnp.int32, (count, count), 1
    )
    before = nn(one_hot(matches), one_hot(earlier))
    return jnp.sum(jnp.where(matches, before, 0.0), axis=0, keepdims=True).astype(jnp.int32)


def placer(target, rows):
    return one_hot(lax.broadcasted_iota(jnp.int32, (rows, target.shape[1]), 0) == target)


def slots_kernel(experts, capacity, give_ref, mixed_ref, slots_ref, target_ref):
    count = mixed_ref.shape[0]
    route = give_ref[count:, :count].astype(jnp.float32)[:1].astype(jnp.int32)
    target = route * (2 * capacity) + slot_numbers(route, experts)
    target_ref[...] = target
    rows = slots_ref.shape[0]
    slots = nn(placer(target, rows), mixed_ref[...])
    slots = slots + nn(placer(target + capacity, rows), give_ref[:count])
    slots_ref[...] = slots.astype(jnp.bfloat16)


def first_rows(slots, capacity):
    column = lax.broadcasted_iota(jnp.int32, (1, slots), 1)
    expert = ((column.astype(jnp.float32) + 0.5) * (1.0 / capacity)).astype(jnp.int32)
    return column + capacity * expert


def unpack_kernel(capacity, sent_ref, x_ref, g_ref):
    sent = sent_ref[...]
    first = first_rows(x_ref.shape[0], capacity)
    x_ref[...] = tn(placer(first, sent.shape[0]), sent).astype(jnp.bfloat16)
    g_ref[...] = tn(placer(first + capacity, sent.shape[0]), sent).astype(jnp.bfloat16)


def unpack(sent, capacity):
    rows, feature = sent.shape
    half = pl.BlockSpec((rows // 2, feature), lambda i: (0, 0))
    return pl.pallas_call(
        functools.partial(unpack_kernel, capacity),
        grid=(1,),
        in_specs=[pl.BlockSpec((rows, feature), lambda i: (0, 0))],
        out_specs=[half] * 2,
        out_shape=[pltpu.HBM((rows // 2, feature), jnp.bfloat16)] * 2,
        compiler_params=pltpu.CompilerParams(vmem_limit_bytes=VMEM_LIMIT),
        cost_estimate=pl.CostEstimate(
            flops=600_000_000, bytes_accessed=1_600_000, transcendentals=0
        ),
        name="unpack",
    )(sent)


def interleave_kernel(capacity, out_ref, in_ref, both_ref):
    rows = both_ref.shape[0]
    first = first_rows(out_ref.shape[0], capacity)
    both = nn(placer(first, rows), out_ref[...]) + nn(placer(first + capacity, rows), in_ref[...])
    both_ref[...] = both.astype(jnp.bfloat16)


def interleave(outs, ins, half, capacity):
    rows, feature = outs.shape
    block = pl.BlockSpec((rows // 2, feature), lambda i: (half, 0))
    return pl.pallas_call(
        functools.partial(interleave_kernel, capacity),
        grid=(1,),
        in_specs=[block] * 2,
        out_specs=pl.BlockSpec((rows, feature), lambda i: (0, 0)),
        out_shape=jax.ShapeDtypeStruct((rows, feature), jnp.bfloat16),
        compiler_params=pltpu.CompilerParams(vmem_limit_bytes=MIDDLE_LIMIT),
        cost_estimate=pl.CostEstimate(
            flops=600_000_000, bytes_accessed=1_600_000, transcendentals=0
        ),
        name="interleave",
    )(outs, ins)


def back_rows_kernel(capacity, target_ref, back_ref, give_ref):
    count, rows = target_ref.shape[1], back_ref.shape[0]
    target = target_ref[...]
    give_ref[:count] = tn(placer(target, rows), back_ref[...]).astype(jnp.bfloat16)
    give_ref[count:] = tn(placer(target + capacity, rows), back_ref[...]).astype(jnp.bfloat16)


def combine_kernel(capacity, target_ref, back_ref, got_ref, mixed_ref, gate_ref, layer_ref, grad_ref):
    f32, bf16 = jnp.float32, jnp.bfloat16
    count, rows = target_ref.shape[1], back_ref.shape[0]
    target = target_ref[...]
    token_out = tn(placer(target, rows), back_ref[...]) + got_ref[:count].astype(f32)
    layer_ref[...] = (mixed_ref[...].astype(f32) + gate_ref[...] * token_out).astype(bf16)
    token_grad = tn(placer(target + capacity, rows), back_ref[...]) + got_ref[count:].astype(f32)
    grad_ref[...] = token_grad.astype(bf16)


def gradients_kernel(scale, sum_ref, up_ref, down_ref):
    width = up_ref.shape[1]
    up_ref[0] = sum_ref[0, :width].astype(jnp.float32) * scale
    down_ref[0] = sum_ref[0, width:].astype(jnp.float32) * scale


def gradients(summed, scale):
    _, rows, feature = summed.shape
    width = rows // 2
    block = pl.BlockSpec((1, width, feature), lambda i: (0, 0, 0))
    return pl.pallas_call(
        functools.partial(gradients_kernel, scale),
        grid=(1,),
        in_specs=[pl.BlockSpec((1, rows, feature), lambda i: (0, 0, 0))],
        out_specs=[block] * 2,
        out_shape=[jax.ShapeDtypeStruct((1, width, feature), jnp.float32)] * 2,
        compiler_params=pltpu.CompilerParams(vmem_limit_bytes=MIDDLE_LIMIT),
        cost_estimate=pl.CostEstimate(flops=1_000_000, bytes_accessed=800_000, transcendentals=0),
        name="gradients",
    )(summed)


def middle_kernel(w_ref, *refs):
    slots, (grads_ref, hid_ref, pg_ref) = refs[:-3], refs[-3:]
    shards, _, width, feature = w_ref.shape
    up = w_ref[:, 0].reshape(shards * width, feature)
    down = w_ref[:, 1].reshape(shards * width, feature)
    rows = slots[0].shape[0]
    halves = len(slots) // 2
    pres = [nt(up, slots[2 * n][...]) for n in range(halves)]
    backs = [nt(down, slots[2 * n + 1][...]) for n in range(halves)]
    grad_up = grad_down = None
    for n in range(halves):
        pre = pres[n]
        square = pre * pre
        inner = jnp.tanh(pre * (GELU_C + (GELU_C * 0.044715) * square))
        half = 0.5 + 0.5 * inner
        hidden = (pre * half).astype(jnp.bfloat16)
        slope = half + (0.5 * pre) * (1.0 - inner * inner) * (
            GELU_C + (3.0 * 0.044715 * GELU_C) * square
        )
        pre_grad = (backs[n] * slope).astype(jnp.bfloat16)
        hid_ref[:, n * rows : (n + 1) * rows] = hidden
        pg_ref[:, n * rows : (n + 1) * rows] = pre_grad
        by_up = nn(pre_grad, slots[2 * n][...])
        by_down = nn(hidden, slots[2 * n + 1][...])
        grad_up = by_up if grad_up is None else grad_up + by_up
        grad_down = by_down if grad_down is None else grad_down + by_down
    grads_ref[:, :width] = grad_up.astype(jnp.bfloat16).reshape(shards, width, feature)
    grads_ref[:, width:] = grad_down.astype(jnp.bfloat16).reshape(shards, width, feature)


def middle(weights, slots):
    owners, _, width, feature = weights.shape
    rows = slots[0].shape[0]
    step = owners // CHUNKS
    ff = owners * width
    total = rows * len(slots) // 2
    return pl.pallas_call(
        middle_kernel,
        grid=(CHUNKS,),
        in_specs=[pl.BlockSpec((step, 2, width, feature), lambda i: (i, 0, 0, 0))]
        + [pl.BlockSpec((rows, feature), lambda i: (0, 0))] * len(slots),
        out_specs=[
            pl.BlockSpec((step, 2 * width, feature), lambda i: (i, 0, 0)),
            pl.BlockSpec((step * width, total), lambda i: (i, 0)),
            pl.BlockSpec((step * width, total), lambda i: (i, 0)),
        ],
        out_shape=[
            pltpu.HBM((owners, 2 * width, feature), jnp.bfloat16),
            pltpu.HBM((ff, total), jnp.bfloat16),
            pltpu.HBM((ff, total), jnp.bfloat16),
        ],
        compiler_params=pltpu.CompilerParams(vmem_limit_bytes=MIDDLE_LIMIT),
        cost_estimate=pl.CostEstimate(
            flops=8 * total * ff * feature,
            bytes_accessed=8 * ff * feature + 4 * ff * total,
            transcendentals=ff * total,
        ),
        name="middle",
    )(weights, *slots)


def back_kernel(side, w_ref, act_ref, out_ref, acc):
    shards, _, width, feature = w_ref.shape
    matrix = w_ref[:, 0].reshape(shards * width, feature)

    @pl.when(pl.program_id(0) == 0)
    def _():
        acc[...] = jnp.zeros_like(acc)

    acc[...] += tn(act_ref[...], matrix)

    @pl.when(pl.program_id(0) == pl.num_programs(0) - 1)
    def _():
        out_ref[...] = acc[...].astype(jnp.bfloat16)


def back(weights, activity, side):
    owners, _, width, feature = weights.shape
    ff, rows = activity.shape
    steps = 2
    step = owners // steps
    return pl.pallas_call(
        functools.partial(back_kernel, side),
        grid=(steps,),
        in_specs=[
            pl.BlockSpec((step, 1, width, feature), lambda i: (i, side, 0, 0)),
            pl.BlockSpec((step * width, rows), lambda i: (i, 0)),
        ],
        out_specs=pl.BlockSpec((rows, feature), lambda i: (0, 0)),
        out_shape=jax.ShapeDtypeStruct((rows, feature), jnp.bfloat16),
        scratch_shapes=[pltpu.VMEM((rows, feature), jnp.float32)],
        compiler_params=pltpu.CompilerParams(vmem_limit_bytes=MIDDLE_LIMIT),
        cost_estimate=pl.CostEstimate(
            flops=2 * rows * ff * feature,
            bytes_accessed=2 * ff * feature + 2 * ff * rows,
            transcendentals=0,
        ),
        name="back",
    )(weights, activity)


def window_index(row, col, tile):
    wins = (tile + 2 * margin_cells) // window_side
    window = (row // window_side) * wins + col // window_side
    return (window * window_side + row % window_side) * window_side + col % window_side


def into_windows(tile):
    ext = tile + 2 * margin_cells
    edge, strip = margin_cells * tile, margin_cells * ext
    piece = lax.broadcasted_iota(jnp.int32, (1, ext * ext), 1)
    base = tile * tile
    row, col = margin_cells + piece // tile, margin_cells + piece % tile
    low = piece - base
    row = jnp.where(piece >= base, low // tile, row)
    high = piece - (base + edge)
    row = jnp.where(piece >= base + edge, tile + margin_cells + high // tile, row)
    left = piece - (base + 2 * edge)
    side = piece >= base + 2 * edge
    row = jnp.where(side, left // margin_cells, row)
    col = jnp.where(side, left % margin_cells, col)
    right = left - strip
    side = piece >= base + 2 * edge + strip
    row = jnp.where(side, right // margin_cells, row)
    col = jnp.where(side, tile + margin_cells + right % margin_cells, col)
    place = window_index(row, col, tile)
    return one_hot(lax.broadcasted_iota(jnp.int32, (ext * ext, ext * ext), 0) == place)


def out_of_windows(tile):
    ext = tile + 2 * margin_cells
    token = lax.broadcasted_iota(jnp.int32, (tile * tile, 1), 0)
    place = window_index(token // tile + margin_cells, token % tile + margin_cells, tile)
    return one_hot(lax.broadcasted_iota(jnp.int32, (tile * tile, ext * ext), 1) == place)


def front_kernel(
    at_ref, tok_ref, low_ref, high_ref, left_ref, right_ref, wqkv_ref, wproj_ref, mixed_ref, qkv_ref, ctx_ref
):
    bf16, f32 = jnp.bfloat16, jnp.float32
    tokens = tok_ref[...]
    count, feature = tokens.shape
    cells = window_side * window_side
    head = feature // HEADS
    group = 128 // head
    pieces = jnp.concatenate(
        [tokens, low_ref[...], high_ref[...], left_ref[...], right_ref[...]], axis=0
    )
    placed = nn(into_windows(math.isqrt(count)), pieces).astype(bf16)
    qkv_ref[...] = jnp.dot(placed, wqkv_ref[...], preferred_element_type=f32).astype(bf16)
    first_row, last_row = at_ref[0] == 0, at_ref[0] == at_ref[1] - 1
    first_col, last_col = at_ref[2] == 0, at_ref[2] == at_ref[3] - 1
    lane = lax.broadcasted_iota(jnp.int32, (1, 128), 1)
    own = [
        ((lane >= h * head) & (lane < (h + 1) * head)).astype(f32) for h in range(group)
    ]
    own16 = [o.astype(bf16) for o in own]
    key = lax.broadcasted_iota(jnp.int32, (cells, 128), 0)
    key_row, key_col = key // window_side, key % window_side
    half = window_side // 2
    low_bias = jnp.float32(-1e30)
    edge_bias = {
        (0, 0): jnp.where(key_row < half, jnp.where(first_row, low_bias, 0.0), 0.0),
        (0, 2): jnp.where(key_row >= half, jnp.where(last_row, low_bias, 0.0), 0.0),
        (1, 0): jnp.where(key_col < half, jnp.where(first_col, low_bias, 0.0), 0.0),
        (1, 2): jnp.where(key_col >= half, jnp.where(last_col, low_bias, 0.0), 0.0),
    }
    scale = 1.0 / math.sqrt(head)
    for window in range(9):
        wi, wj = window // 3, window % 3
        bias = None
        if wi != 1:
            bias = edge_bias[0, wi]
        if wj != 1:
            bias = edge_bias[1, wj] if bias is None else bias + edge_bias[1, wj]
        if bias is not None:
            bias = jnp.concatenate([bias] * (group * cells // 128), axis=1)
        rows = slice(window * cells, (window + 1) * cells)
        for g in range(feature // 128):
            q = qkv_ref[rows, g * 128 : (g + 1) * 128]
            k = qkv_ref[rows, feature + g * 128 : feature + (g + 1) * 128]
            v = qkv_ref[rows, 2 * feature + g * 128 : 2 * feature + (g + 1) * 128]
            spread = jnp.concatenate([q * o for o in own16], axis=0)
            scores = nt(k, spread)
            if bias is not None:
                scores = scores + bias
            peak = jnp.max(scores, axis=0, keepdims=True)
            weights = jnp.exp((scores - peak) * scale)
            probs = (weights * (1.0 / jnp.sum(weights, axis=0, keepdims=True))).astype(bf16)
            wide = tn(probs, v)
            mine = wide[:cells] * own[0]
            for h in range(1, group):
                mine = mine + wide[h * cells : (h + 1) * cells] * own[h]
            ctx_ref[rows, g * 128 : (g + 1) * 128] = mine.astype(bf16)
    context = nn(out_of_windows(math.isqrt(count)), ctx_ref[...]).astype(bf16)
    attended = jnp.dot(context, wproj_ref[...], preferred_element_type=f32)
    centred = attended - jnp.mean(attended, axis=-1, keepdims=True)
    spread_of = jnp.mean(centred * centred, axis=-1, keepdims=True)
    mixed = (tokens.astype(f32) + centred * lax.rsqrt(spread_of + 1e-05)).astype(bf16)
    mixed_ref[...] = mixed


def front(at, tokens, low, high, left, right, w_qkv, w_proj):
    count, feature = tokens.shape
    ext = (math.isqrt(count) + 2 * margin_cells) ** 2
    smem = pl.BlockSpec(memory_space=pltpu.SMEM)
    vmem = pl.BlockSpec(memory_space=pltpu.VMEM)
    return vmem_call(
        front_kernel,
        [((count, feature), jnp.bfloat16)],
        "front",
        4_000_000_000,
        in_specs=[smem] + [vmem] * 7,
        scratch_shapes=[
            pltpu.VMEM((ext, 3 * feature), jnp.bfloat16),
            pltpu.VMEM((ext, feature), jnp.bfloat16),
        ],
    )(at, tokens, low, high, left, right, w_qkv, w_proj)[0]


def shifts(axis):
    count = lax.axis_size(axis)
    forward = [(i, i + 1) for i in range(count - 1)]
    return forward, [(target, source) for source, target in forward]


def sharing():
    count, width = lax.axis_size("rep"), lax.axis_size("exp")
    groups = [list(range(parity, count, 2)) for parity in range(2)]
    swap = []
    for rep in range(count):
        for exp in range(width):
            partner = (rep + 1) % count if (rep + exp) % 2 == 0 else (rep - 1) % count
            swap.append((rep * width + exp, partner * width + exp))
    return groups, swap


def per_device(tokens, gate, route, cotangent, w_qkv, w_proj, w_up, w_down):
    tile_rows, tile_cols, feature = tokens.shape
    tok_count = tile_rows * tile_cols
    margin = margin_cells
    experts = lax.axis_size("exp")
    capacity = max(2, 3 * tok_count // (2 * experts))
    slot_count = 2 * experts * capacity
    bf16, f32 = jnp.bfloat16, jnp.float32
    rows_of = ((slot_count, feature), bf16)
    groups, swap = sharing()

    def exchange(rows):
        return lax.ppermute(rows, ("rep", "exp"), swap)

    def dispatch(rows):
        blocks = rows.reshape(experts, -1, feature)
        return lax.all_to_all(blocks, "exp", 0, 0, tiled=True).reshape(-1, feature)

    weights = lax.all_gather(
        jnp.concatenate([w_up, w_down], axis=0),
        "rep",
        axis=0,
        tiled=False,
        axis_index_groups=groups,
    )
    forward, backward = shifts("rep")
    low = lax.ppermute(tokens[tile_rows - margin :], "rep", forward)
    high = lax.ppermute(tokens[:margin], "rep", backward)
    gate_rows = gate.reshape(tok_count, 1)
    [give] = vmem_call(
        upstream_kernel, [((tok_count + EXTRA, feature), bf16)], "upstream", 1_000_000, count=3
    )(route.reshape(1, tok_count), gate_rows, cotangent.reshape(tok_count, feature))
    got = exchange(give)
    forward, backward = shifts("exp")

    def strip(cols):
        parts = [low[:, cols], tokens[:, cols], high[:, cols]]
        return jnp.concatenate(parts, axis=0).reshape(-1, feature)

    left = lax.ppermute(strip(slice(tile_cols - margin, tile_cols)), "exp", forward)
    right = lax.ppermute(strip(slice(0, margin)), "exp", backward)
    left, got = lax.optimization_barrier((left, got))
    at = jnp.stack(
        [
            lax.axis_index("rep"),
            jnp.int32(lax.axis_size("rep")),
            lax.axis_index("exp"),
            jnp.int32(experts),
        ]
    ).astype(jnp.int32)
    mixed = front(
        at,
        tokens.reshape(tok_count, feature),
        low.reshape(-1, feature),
        high.reshape(-1, feature),
        left,
        right,
        w_qkv,
        w_proj,
    )
    got_mixed = exchange(mixed)

    def dispatched(side, features):
        slots, target = vmem_call(
            functools.partial(slots_kernel, experts, capacity),
            [rows_of, ((1, tok_count), jnp.int32)],
            "slots",
            500_000_000,
            count=2,
        )(side, features)
        return unpack(dispatch(slots), capacity), target

    own_parts, target = dispatched(give, mixed)
    other_parts, other_target = dispatched(got, got_mixed)
    grads, hidden, pre_grad = middle(weights, [*own_parts, *other_parts])
    summed = lax.psum_scatter(
        grads, "rep", scatter_dimension=0, tiled=True, axis_index_groups=groups
    )

    outs, ins = back(weights, hidden, 1), back(weights, pre_grad, 0)
    back_other = dispatch(interleave(outs, ins, 1, capacity))
    [theirs] = vmem_call(
        functools.partial(back_rows_kernel, capacity),
        [((2 * tok_count, feature), bf16)],
        "back_rows",
        400_000_000,
        count=2,
    )(other_target, back_other)
    outs, back_other = lax.optimization_barrier((outs, back_other))
    back_own = dispatch(interleave(outs, ins, 0, capacity))
    layer_out, input_grad = vmem_call(
        functools.partial(combine_kernel, capacity),
        [((tok_count, feature), bf16)] * 2,
        "combine",
        400_000_000,
        count=5,
    )(target, back_own, exchange(theirs), mixed, gate_rows)
    grad_up, grad_down = gradients(summed, 1.0 / lax.axis_size("rep"))
    return (
        layer_out.reshape(tile_rows, tile_cols, feature),
        input_grad.reshape(tile_rows, tile_cols, feature),
        grad_up,
        grad_down,
    )


def solution(mesh):
    placed = (
        P("rep", "exp", None),
        P("rep", "exp"),
        P("rep", "exp", None, None),
        P("rep", "exp", None),
        P(),
        P(),
        P("exp", "rep", None),
        P("exp", "rep", None),
    )
    return jax.shard_map(
        per_device,
        mesh=mesh,
        in_specs=placed,
        out_specs=(
            P("rep", "exp", None),
            P("rep", "exp", None),
            P("exp", "rep", None),
            P("exp", "rep", None),
        ),
        check_vma=False,
    )
```

```python
import functools
import math

import jax
import jax.numpy as jnp
from jax import lax
from jax.experimental import pallas as pl
from jax.experimental.pallas import tpu as pltpu
from jax.sharding import PartitionSpec as P

HEADS = 16


GELU_C = math.sqrt(2.0 / math.pi)
window_side = 8
margin_cells = 4
CHUNKS = 4
EXTRA = 16

VMEM_LIMIT = 24 * 1024 * 1024
MIDDLE_LIMIT = 58 * 1024 * 1024


def nt(a, b):
    return lax.dot_general(a, b, (((1,), (1,)), ((), ())), preferred_element_type=jnp.float32)


def tn(a, b):
    return lax.dot_general(a, b, (((0,), (0,)), ((), ())), preferred_element_type=jnp.float32)


def nn(a, b):
    return jnp.dot(a, b, preferred_element_type=jnp.float32)


def one_hot(mask):
    return mask.astype(jnp.float32).astype(jnp.bfloat16)


def vmem_call(kernel, out, name, flops, in_specs=None, count=0, **more):
    vmem = pl.BlockSpec(memory_space=pltpu.VMEM)
    return pl.pallas_call(
        kernel,
        in_specs=in_specs or [vmem] * count,
        out_specs=[vmem] * len(out),
        out_shape=[jax.ShapeDtypeStruct(shape, dtype) for shape, dtype in out],
        compiler_params=pltpu.CompilerParams(vmem_limit_bytes=VMEM_LIMIT),
        cost_estimate=pl.CostEstimate(flops=flops, bytes_accessed=3_000_000, transcendentals=0),
        name=name,
        **more,
    )


def upstream_kernel(route_ref, gate_ref, cot_ref, give_ref):
    f32, bf16 = jnp.float32, jnp.bfloat16
    count, feature = cot_ref.shape
    give_ref[:count] = (gate_ref[...] * cot_ref[...].astype(f32)).astype(bf16)
    route = route_ref[...].astype(f32)
    row = jnp.concatenate([route, jnp.zeros((1, feature - count), f32)], axis=1)
    extra = give_ref.shape[0] - count
    give_ref[count:] = jnp.broadcast_to(row, (extra, feature)).astype(bf16)


def slot_numbers(route, experts):
    count = route.shape[1]
    matches = lax.broadcasted_iota(jnp.int32, (experts, count), 0) == route
    earlier = lax.broadcasted_iota(jnp.int32, (count, count), 0) < lax.broadcasted_iota(
        jnp.int32, (count, count), 1
    )
    before = nn(one_hot(matches), one_hot(earlier))
    return jnp.sum(jnp.where(matches, before, 0.0), axis=0, keepdims=True).astype(jnp.int32)


def placer(target, rows):
    return one_hot(lax.broadcasted_iota(jnp.int32, (rows, target.shape[1]), 0) == target)


def grad_slots_kernel(experts, capacity, give_ref, got_ref, slots_ref, target_ref):
    feature = give_ref.shape[1]
    count = give_ref.shape[0] - EXTRA
    total = None
    for n, ref in enumerate((give_ref, got_ref)):
        route = ref[count:, :count].astype(jnp.float32)[:1].astype(jnp.int32)
        target = route * (2 * capacity) + n * capacity + slot_numbers(route, experts)
        target_ref[n : n + 1] = target
        placed = nn(placer(target, 2 * experts * capacity), ref[:count])
        total = placed if total is None else total + placed
    slots_ref[...] = total.astype(jnp.bfloat16)


def token_slots_kernel(target_ref, mixed_ref, first_ref, second_ref, slots_ref):
    rows = slots_ref.shape[0]
    total = nn(placer(target_ref[0:1], rows), mixed_ref[...])
    got = jnp.concatenate([first_ref[...], second_ref[...]], axis=0)
    total = total + nn(placer(target_ref[1:2], rows), got)
    slots_ref[...] = total.astype(jnp.bfloat16)


def back_rows_kernel(target_ref, back_ref, give_ref):
    give_ref[...] = tn(placer(target_ref[1:2], back_ref.shape[0]), back_ref[...]).astype(
        jnp.bfloat16
    )


def combine_kernel(
    target_ref, out_ref, got_out_ref, in_ref, got_in_ref, mixed_ref, gate_ref, layer_ref, grad_ref
):
    f32, bf16 = jnp.float32, jnp.bfloat16
    mine = placer(target_ref[0:1], out_ref.shape[0])
    token_out = tn(mine, out_ref[...]) + got_out_ref[...].astype(f32)
    layer_ref[...] = (mixed_ref[...].astype(f32) + gate_ref[...] * token_out).astype(bf16)
    grad_ref[...] = (tn(mine, in_ref[...]) + got_in_ref[...].astype(f32)).astype(bf16)


def gradients_kernel(scale, sum_ref, up_ref, down_ref):
    width = up_ref.shape[1]
    up_ref[0] = sum_ref[0, :width].astype(jnp.float32) * scale
    down_ref[0] = sum_ref[0, width:].astype(jnp.float32) * scale


def middle_kernel(w_ref, x_ref, g_ref, grads_ref, hid_ref, pg_ref):
    shards, _, width, feature = w_ref.shape
    up = w_ref[:, 0].reshape(shards * width, feature)
    down = w_ref[:, 1].reshape(shards * width, feature)
    halves = 2
    rows = x_ref.shape[0] // halves
    parts = [slice(n * rows, (n + 1) * rows) for n in range(halves)]
    pres = [nt(up, x_ref[part]) for part in parts]
    backs = [nt(down, g_ref[part]) for part in parts]
    grad_up = grad_down = None
    for n, part in enumerate(parts):
        pre = pres[n]
        square = pre * pre
        inner = jnp.tanh(pre * (GELU_C + (GELU_C * 0.044715) * square))
        half = 0.5 + 0.5 * inner
        hidden = (pre * half).astype(jnp.bfloat16)
        slope = half + (0.5 * pre) * (1.0 - inner * inner) * (
            GELU_C + (3.0 * 0.044715 * GELU_C) * square
        )
        pre_grad = (backs[n] * slope).astype(jnp.bfloat16)
        hid_ref[:, part] = hidden
        pg_ref[:, part] = pre_grad
        by_up = nn(pre_grad, x_ref[part])
        by_down = nn(hidden, g_ref[part])
        grad_up = by_up if grad_up is None else grad_up + by_up
        grad_down = by_down if grad_down is None else grad_down + by_down
    grads_ref[:, :width] = grad_up.astype(jnp.bfloat16).reshape(shards, width, feature)
    grads_ref[:, width:] = grad_down.astype(jnp.bfloat16).reshape(shards, width, feature)


def middle(weights, slot_x, slot_g):
    owners, _, width, feature = weights.shape
    rows = slot_x.shape[0]
    step = owners // CHUNKS
    ff = owners * width
    return pl.pallas_call(
        middle_kernel,
        grid=(CHUNKS,),
        in_specs=[
            pl.BlockSpec((step, 2, width, feature), lambda i: (i, 0, 0, 0)),
            pl.BlockSpec((rows, feature), lambda i: (0, 0)),
            pl.BlockSpec((rows, feature), lambda i: (0, 0)),
        ],
        out_specs=[
            pl.BlockSpec((step, 2 * width, feature), lambda i: (i, 0, 0)),
            pl.BlockSpec((step * width, rows), lambda i: (i, 0)),
            pl.BlockSpec((step * width, rows), lambda i: (i, 0)),
        ],
        out_shape=[
            pltpu.HBM((owners, 2 * width, feature), jnp.bfloat16),
            pltpu.HBM((ff, rows), jnp.bfloat16),
            pltpu.HBM((ff, rows), jnp.bfloat16),
        ],
        compiler_params=pltpu.CompilerParams(vmem_limit_bytes=MIDDLE_LIMIT),
        cost_estimate=pl.CostEstimate(
            flops=8 * rows * ff * feature,
            bytes_accessed=8 * ff * feature + 4 * ff * rows,
            transcendentals=ff * rows,
        ),
        name="middle",
    )(weights, slot_x, slot_g)


def back_kernel(side, w_ref, act_ref, out_ref, acc):
    shards, _, width, feature = w_ref.shape
    matrix = w_ref[:, 0].reshape(shards * width, feature)

    @pl.when(pl.program_id(0) == 0)
    def _():
        acc[...] = jnp.zeros_like(acc)

    acc[...] += tn(act_ref[...], matrix)

    @pl.when(pl.program_id(0) == pl.num_programs(0) - 1)
    def _():
        out_ref[...] = acc[...].astype(jnp.bfloat16)


def back(weights, activity, side):
    owners, _, width, feature = weights.shape
    ff, rows = activity.shape
    steps = 2
    step = owners // steps
    return pl.pallas_call(
        functools.partial(back_kernel, side),
        grid=(steps,),
        in_specs=[
            pl.BlockSpec((step, 1, width, feature), lambda i: (i, side, 0, 0)),
            pl.BlockSpec((step * width, rows), lambda i: (i, 0)),
        ],
        out_specs=pl.BlockSpec((rows, feature), lambda i: (0, 0)),
        out_shape=jax.ShapeDtypeStruct((rows, feature), jnp.bfloat16),
        scratch_shapes=[pltpu.VMEM((rows, feature), jnp.float32)],
        compiler_params=pltpu.CompilerParams(vmem_limit_bytes=MIDDLE_LIMIT),
        cost_estimate=pl.CostEstimate(
            flops=2 * rows * ff * feature,
            bytes_accessed=2 * ff * feature + 2 * ff * rows,
            transcendentals=0,
        ),
        name="back",
    )(weights, activity)


def window_index(row, col, tile):
    wins = (tile + 2 * margin_cells) // window_side
    window = (row // window_side) * wins + col // window_side
    return (window * window_side + row % window_side) * window_side + col % window_side


def into_windows(tile):
    ext = tile + 2 * margin_cells
    edge, strip = margin_cells * tile, margin_cells * ext
    piece = lax.broadcasted_iota(jnp.int32, (1, ext * ext), 1)
    base = tile * tile
    row, col = margin_cells + piece // tile, margin_cells + piece % tile
    low = piece - base
    row = jnp.where(piece >= base, low // tile, row)
    high = piece - (base + edge)
    row = jnp.where(piece >= base + edge, tile + margin_cells + high // tile, row)
    left = piece - (base + 2 * edge)
    side = piece >= base + 2 * edge
    row = jnp.where(side, left // margin_cells, row)
    col = jnp.where(side, left % margin_cells, col)
    right = left - strip
    side = piece >= base + 2 * edge + strip
    row = jnp.where(side, right // margin_cells, row)
    col = jnp.where(side, tile + margin_cells + right % margin_cells, col)
    place = window_index(row, col, tile)
    return one_hot(lax.broadcasted_iota(jnp.int32, (ext * ext, ext * ext), 0) == place)


def out_of_windows(tile):
    ext = tile + 2 * margin_cells
    token = lax.broadcasted_iota(jnp.int32, (tile * tile, 1), 0)
    place = window_index(token // tile + margin_cells, token % tile + margin_cells, tile)
    return one_hot(lax.broadcasted_iota(jnp.int32, (tile * tile, ext * ext), 1) == place)


def front_kernel(
    at_ref, tok_ref, low_ref, high_ref, left_ref, right_ref, wqkv_ref, wproj_ref,
    mixed_ref, first_ref, second_ref, qkv_ref, ctx_ref,
):
    bf16, f32 = jnp.bfloat16, jnp.float32
    tokens = tok_ref[...]
    count, feature = tokens.shape
    cells = window_side * window_side
    head = feature // HEADS
    group = 128 // head
    pieces = jnp.concatenate(
        [tokens, low_ref[...], high_ref[...], left_ref[...], right_ref[...]], axis=0
    )
    placed = nn(into_windows(math.isqrt(count)), pieces).astype(bf16)
    qkv_ref[...] = jnp.dot(placed, wqkv_ref[...], preferred_element_type=f32).astype(bf16)
    first_row, last_row = at_ref[0] == 0, at_ref[0] == at_ref[1] - 1
    first_col, last_col = at_ref[2] == 0, at_ref[2] == at_ref[3] - 1
    lane = lax.broadcasted_iota(jnp.int32, (1, 128), 1)
    own = [
        ((lane >= h * head) & (lane < (h + 1) * head)).astype(f32) for h in range(group)
    ]
    own16 = [o.astype(bf16) for o in own]
    key = lax.broadcasted_iota(jnp.int32, (cells, 128), 0)
    key_row, key_col = key // window_side, key % window_side
    half = window_side // 2
    low_bias = jnp.float32(-1e30)
    edge_bias = {
        (0, 0): jnp.where(key_row < half, jnp.where(first_row, low_bias, 0.0), 0.0),
        (0, 2): jnp.where(key_row >= half, jnp.where(last_row, low_bias, 0.0), 0.0),
        (1, 0): jnp.where(key_col < half, jnp.where(first_col, low_bias, 0.0), 0.0),
        (1, 2): jnp.where(key_col >= half, jnp.where(last_col, low_bias, 0.0), 0.0),
    }
    scale = 1.0 / math.sqrt(head)
    for window in range(9):
        wi, wj = window // 3, window % 3
        bias = None
        if wi != 1:
            bias = edge_bias[0, wi]
        if wj != 1:
            bias = edge_bias[1, wj] if bias is None else bias + edge_bias[1, wj]
        if bias is not None:
            bias = jnp.concatenate([bias] * (group * cells // 128), axis=1)
        rows = slice(window * cells, (window + 1) * cells)
        for g in range(feature // 128):
            q = qkv_ref[rows, g * 128 : (g + 1) * 128]
            k = qkv_ref[rows, feature + g * 128 : feature + (g + 1) * 128]
            v = qkv_ref[rows, 2 * feature + g * 128 : 2 * feature + (g + 1) * 128]
            spread = jnp.concatenate([q * o for o in own16], axis=0)
            scores = nt(k, spread)
            if bias is not None:
                scores = scores + bias
            peak = jnp.max(scores, axis=0, keepdims=True)
            weights = jnp.exp((scores - peak) * scale)
            probs = (weights * (1.0 / jnp.sum(weights, axis=0, keepdims=True))).astype(bf16)
            wide = tn(probs, v)
            mine = wide[:cells] * own[0]
            for h in range(1, group):
                mine = mine + wide[h * cells : (h + 1) * cells] * own[h]
            ctx_ref[rows, g * 128 : (g + 1) * 128] = mine.astype(bf16)
    context = nn(out_of_windows(math.isqrt(count)), ctx_ref[...]).astype(bf16)
    attended = jnp.dot(context, wproj_ref[...], preferred_element_type=f32)
    centred = attended - jnp.mean(attended, axis=-1, keepdims=True)
    spread_of = jnp.mean(centred * centred, axis=-1, keepdims=True)
    mixed = (tokens.astype(f32) + centred * lax.rsqrt(spread_of + 1e-05)).astype(bf16)
    mixed_ref[...] = mixed
    for n, ref in enumerate((first_ref, second_ref)):
        ref[...] = mixed[n * count // 2 : (n + 1) * count // 2]


def front(at, tokens, low, high, left, right, w_qkv, w_proj):
    count, feature = tokens.shape
    ext = (math.isqrt(count) + 2 * margin_cells) ** 2
    smem = pl.BlockSpec(memory_space=pltpu.SMEM)
    vmem = pl.BlockSpec(memory_space=pltpu.VMEM)
    return vmem_call(
        front_kernel,
        [((count, feature), jnp.bfloat16)] + [((count // 2, feature), jnp.bfloat16)] * 2,
        "front",
        4_000_000_000,
        in_specs=[smem] + [vmem] * 7,
        scratch_shapes=[
            pltpu.VMEM((ext, 3 * feature), jnp.bfloat16),
            pltpu.VMEM((ext, feature), jnp.bfloat16),
        ],
    )(at, tokens, low, high, left, right, w_qkv, w_proj)


def shifts(axis):
    count = lax.axis_size(axis)
    forward = [(i, i + 1) for i in range(count - 1)]
    return forward, [(target, source) for source, target in forward]


def sharing():
    count, width = lax.axis_size("rep"), lax.axis_size("exp")
    groups = [list(range(parity, count, 2)) for parity in range(2)]
    swap = []
    for rep in range(count):
        for exp in range(width):
            partner = (rep + 1) % count if (rep + exp) % 2 == 0 else (rep - 1) % count
            swap.append((rep * width + exp, partner * width + exp))
    return groups, swap


def per_device(tokens, gate, route, cotangent, w_qkv, w_proj, w_up, w_down):
    tile_rows, tile_cols, feature = tokens.shape
    tok_count = tile_rows * tile_cols
    margin = margin_cells
    experts = lax.axis_size("exp")
    capacity = max(2, 3 * tok_count // (2 * experts))
    slot_count = 2 * experts * capacity
    bf16, f32 = jnp.bfloat16, jnp.float32
    rows_of = ((slot_count, feature), bf16)
    groups, swap = sharing()

    def exchange(rows):
        return lax.ppermute(rows, ("rep", "exp"), swap)

    def dispatch(rows):
        blocks = rows.reshape(experts, -1, feature)
        return lax.all_to_all(blocks, "exp", 0, 0, tiled=True).reshape(-1, feature)

    weights = lax.all_gather(
        jnp.concatenate([w_up, w_down], axis=0),
        "rep",
        axis=0,
        tiled=False,
        axis_index_groups=groups,
    )
    forward, backward = shifts("rep")
    low = lax.ppermute(tokens[tile_rows - margin :], "rep", forward)
    high = lax.ppermute(tokens[:margin], "rep", backward)
    gate_rows = gate.reshape(tok_count, 1)
    [give] = vmem_call(
        upstream_kernel, [((tok_count + EXTRA, feature), bf16)], "upstream", 1_000_000, count=3
    )(route.reshape(1, tok_count), gate_rows, cotangent.reshape(tok_count, feature))
    got = exchange(give)
    forward, backward = shifts("exp")

    def strip(cols):
        parts = [low[:, cols], tokens[:, cols], high[:, cols]]
        return jnp.concatenate(parts, axis=0).reshape(-1, feature)

    left = lax.ppermute(strip(slice(tile_cols - margin, tile_cols)), "exp", forward)
    right = lax.ppermute(strip(slice(0, margin)), "exp", backward)
    got, left, right = lax.optimization_barrier((got, left, right))
    at = jnp.stack(
        [
            lax.axis_index("rep"),
            jnp.int32(lax.axis_size("rep")),
            lax.axis_index("exp"),
            jnp.int32(experts),
        ]
    ).astype(jnp.int32)
    mixed, *halves = front(
        at,
        tokens.reshape(tok_count, feature),
        low.reshape(-1, feature),
        high.reshape(-1, feature),
        left,
        right,
        w_qkv,
        w_proj,
    )
    got_halves = [exchange(half) for half in halves]
    slots_g, target = vmem_call(
        functools.partial(grad_slots_kernel, experts, capacity),
        [rows_of, ((2, tok_count), jnp.int32)],
        "grad_slots",
        500_000_000,
        count=2,
    )(give, got)
    slot_g = dispatch(slots_g)
    [slots_x] = vmem_call(token_slots_kernel, [rows_of], "token_slots", 400_000_000, count=4)(
        target, mixed, *got_halves
    )
    slot_x = dispatch(slots_x)
    grads, hidden, pre_grad = middle(weights, slot_x, slot_g)
    summed = lax.psum_scatter(
        grads, "rep", scatter_dimension=0, tiled=True, axis_index_groups=groups
    )

    def exchanged(rows):
        [theirs] = vmem_call(
            back_rows_kernel, [((tok_count, feature), bf16)], "back_rows", 200_000_000, count=2
        )(target, rows)
        return exchange(theirs)

    back_out = dispatch(back(weights, hidden, 1))
    back_in = dispatch(back(weights, pre_grad, 0))
    got_out = exchanged(back_out)
    back_in, got_out = lax.optimization_barrier((back_in, got_out))
    layer_out, input_grad = vmem_call(
        combine_kernel, [((tok_count, feature), bf16)] * 2, "combine", 400_000_000, count=7
    )(target, back_out, got_out, back_in, exchanged(back_in), mixed, gate_rows)
    grad_up, grad_down = vmem_call(
        functools.partial(gradients_kernel, 1.0 / lax.axis_size("rep")),
        [(w_up.shape, f32)] * 2,
        "gradients",
        1_000_000,
        count=1,
    )(summed)
    return (
        layer_out.reshape(tile_rows, tile_cols, feature),
        input_grad.reshape(tile_rows, tile_cols, feature),
        grad_up,
        grad_down,
    )


def solution(mesh):
    placed = (
        P("rep", "exp", None),
        P("rep", "exp"),
        P("rep", "exp", None, None),
        P("rep", "exp", None),
        P(),
        P(),
        P("exp", "rep", None),
        P("exp", "rep", None),
    )
    return jax.shard_map(
        per_device,
        mesh=mesh,
        in_specs=placed,
        out_specs=(
            P("rep", "exp", None),
            P("rep", "exp", None),
            P("exp", "rep", None),
            P("exp", "rep", None),
        ),
        check_vma=False,
    )
```

```python
import functools
import math

import jax
import jax.numpy as jnp
from jax import lax
from jax.experimental import pallas as pl
from jax.experimental.pallas import tpu as pltpu
from jax.sharding import PartitionSpec as P

HEADS = 16


GELU_C = math.sqrt(2.0 / math.pi)
window_side = 8
margin_cells = 4
CHUNKS = 4
EXTRA = 16

VMEM_LIMIT = 24 * 1024 * 1024
MIDDLE_LIMIT = 58 * 1024 * 1024


def nt(a, b):
    return lax.dot_general(a, b, (((1,), (1,)), ((), ())), preferred_element_type=jnp.float32)


def tn(a, b):
    return lax.dot_general(a, b, (((0,), (0,)), ((), ())), preferred_element_type=jnp.float32)


def nn(a, b):
    return jnp.dot(a, b, preferred_element_type=jnp.float32)


def one_hot(mask):
    return mask.astype(jnp.float32).astype(jnp.bfloat16)


def vmem_call(kernel, out, name, flops, in_specs=None, count=0, **more):
    vmem = pl.BlockSpec(memory_space=pltpu.VMEM)
    return pl.pallas_call(
        kernel,
        in_specs=in_specs or [vmem] * count,
        out_specs=[vmem] * len(out),
        out_shape=[jax.ShapeDtypeStruct(shape, dtype) for shape, dtype in out],
        compiler_params=pltpu.CompilerParams(vmem_limit_bytes=VMEM_LIMIT),
        cost_estimate=pl.CostEstimate(flops=flops, bytes_accessed=3_000_000, transcendentals=0),
        name=name,
        **more,
    )


def upstream_kernel(route_ref, gate_ref, cot_ref, give_ref):
    f32, bf16 = jnp.float32, jnp.bfloat16
    count, feature = cot_ref.shape
    give_ref[:count] = (gate_ref[...] * cot_ref[...].astype(f32)).astype(bf16)
    route = route_ref[...].astype(f32)
    row = jnp.concatenate([route, jnp.zeros((1, feature - count), f32)], axis=1)
    extra = give_ref.shape[0] - count
    give_ref[count:] = jnp.broadcast_to(row, (extra, feature)).astype(bf16)


def slot_numbers(route, experts):
    count = route.shape[1]
    matches = lax.broadcasted_iota(jnp.int32, (experts, count), 0) == route
    earlier = lax.broadcasted_iota(jnp.int32, (count, count), 0) < lax.broadcasted_iota(
        jnp.int32, (count, count), 1
    )
    before = nn(one_hot(matches), one_hot(earlier))
    return jnp.sum(jnp.where(matches, before, 0.0), axis=0, keepdims=True).astype(jnp.int32)


def placer(target, rows):
    return one_hot(lax.broadcasted_iota(jnp.int32, (rows, target.shape[1]), 0) == target)


def grad_slots_kernel(experts, capacity, give_ref, got_ref, slots_ref, target_ref):
    feature = give_ref.shape[1]
    count = give_ref.shape[0] - EXTRA
    total = None
    for n, ref in enumerate((give_ref, got_ref)):
        route = ref[count:, :count].astype(jnp.float32)[:1].astype(jnp.int32)
        target = route * (2 * capacity) + n * capacity + slot_numbers(route, experts)
        target_ref[n : n + 1] = target
        placed = nn(placer(target, 2 * experts * capacity), ref[:count])
        total = placed if total is None else total + placed
    slots_ref[...] = total.astype(jnp.bfloat16)


def token_slots_kernel(target_ref, mixed_ref, got_ref, slots_ref):
    rows = slots_ref.shape[0]
    total = nn(placer(target_ref[0:1], rows), mixed_ref[...])
    total = total + nn(placer(target_ref[1:2], rows), got_ref[...])
    slots_ref[...] = total.astype(jnp.bfloat16)


def back_rows_kernel(target_ref, back_ref, give_ref):
    give_ref[...] = tn(placer(target_ref[1:2], back_ref.shape[0]), back_ref[...]).astype(
        jnp.bfloat16
    )


def combine_kernel(
    target_ref, out_ref, got_out_ref, in_ref, got_in_ref, mixed_ref, gate_ref, layer_ref, grad_ref
):
    f32, bf16 = jnp.float32, jnp.bfloat16
    mine = placer(target_ref[0:1], out_ref.shape[0])
    token_out = tn(mine, out_ref[...]) + got_out_ref[...].astype(f32)
    layer_ref[...] = (mixed_ref[...].astype(f32) + gate_ref[...] * token_out).astype(bf16)
    grad_ref[...] = (tn(mine, in_ref[...]) + got_in_ref[...].astype(f32)).astype(bf16)


def gradients_kernel(scale, sum_ref, up_ref, down_ref):
    width = up_ref.shape[1]
    up_ref[0] = sum_ref[0, :width].astype(jnp.float32) * scale
    down_ref[0] = sum_ref[0, width:].astype(jnp.float32) * scale


def middle_kernel(w_ref, x_ref, g_ref, grads_ref, hid_ref, pg_ref):
    shards, _, width, feature = w_ref.shape
    up = w_ref[:, 0].reshape(shards * width, feature)
    down = w_ref[:, 1].reshape(shards * width, feature)
    halves = 2
    rows = x_ref.shape[0] // halves
    parts = [slice(n * rows, (n + 1) * rows) for n in range(halves)]
    pres = [nt(up, x_ref[part]) for part in parts]
    backs = [nt(down, g_ref[part]) for part in parts]
    grad_up = grad_down = None
    for n, part in enumerate(parts):
        pre = pres[n]
        square = pre * pre
        inner = jnp.tanh(pre * (GELU_C + (GELU_C * 0.044715) * square))
        half = 0.5 + 0.5 * inner
        hidden = (pre * half).astype(jnp.bfloat16)
        slope = half + (0.5 * pre) * (1.0 - inner * inner) * (
            GELU_C + (3.0 * 0.044715 * GELU_C) * square
        )
        pre_grad = (backs[n] * slope).astype(jnp.bfloat16)
        hid_ref[:, part] = hidden
        pg_ref[:, part] = pre_grad
        by_up = nn(pre_grad, x_ref[part])
        by_down = nn(hidden, g_ref[part])
        grad_up = by_up if grad_up is None else grad_up + by_up
        grad_down = by_down if grad_down is None else grad_down + by_down
    grads_ref[:, :width] = grad_up.astype(jnp.bfloat16).reshape(shards, width, feature)
    grads_ref[:, width:] = grad_down.astype(jnp.bfloat16).reshape(shards, width, feature)


def middle(weights, slot_x, slot_g):
    owners, _, width, feature = weights.shape
    rows = slot_x.shape[0]
    step = owners // CHUNKS
    ff = owners * width
    return pl.pallas_call(
        middle_kernel,
        grid=(CHUNKS,),
        in_specs=[
            pl.BlockSpec((step, 2, width, feature), lambda i: (i, 0, 0, 0)),
            pl.BlockSpec((rows, feature), lambda i: (0, 0)),
            pl.BlockSpec((rows, feature), lambda i: (0, 0)),
        ],
        out_specs=[
            pl.BlockSpec((step, 2 * width, feature), lambda i: (i, 0, 0)),
            pl.BlockSpec((step * width, rows), lambda i: (i, 0)),
            pl.BlockSpec((step * width, rows), lambda i: (i, 0)),
        ],
        out_shape=[
            pltpu.HBM((owners, 2 * width, feature), jnp.bfloat16),
            pltpu.HBM((ff, rows), jnp.bfloat16),
            pltpu.HBM((ff, rows), jnp.bfloat16),
        ],
        compiler_params=pltpu.CompilerParams(vmem_limit_bytes=MIDDLE_LIMIT),
        cost_estimate=pl.CostEstimate(
            flops=8 * rows * ff * feature,
            bytes_accessed=8 * ff * feature + 4 * ff * rows,
            transcendentals=ff * rows,
        ),
        name="middle",
    )(weights, slot_x, slot_g)


def back_kernel(side, w_ref, act_ref, out_ref, acc):
    shards, _, width, feature = w_ref.shape
    matrix = w_ref[:, 0].reshape(shards * width, feature)

    @pl.when(pl.program_id(0) == 0)
    def _():
        acc[...] = jnp.zeros_like(acc)

    acc[...] += tn(act_ref[...], matrix)

    @pl.when(pl.program_id(0) == pl.num_programs(0) - 1)
    def _():
        out_ref[...] = acc[...].astype(jnp.bfloat16)


def back(weights, activity, side):
    owners, _, width, feature = weights.shape
    ff, rows = activity.shape
    steps = 2
    step = owners // steps
    return pl.pallas_call(
        functools.partial(back_kernel, side),
        grid=(steps,),
        in_specs=[
            pl.BlockSpec((step, 1, width, feature), lambda i: (i, side, 0, 0)),
            pl.BlockSpec((step * width, rows), lambda i: (i, 0)),
        ],
        out_specs=pl.BlockSpec((rows, feature), lambda i: (0, 0)),
        out_shape=jax.ShapeDtypeStruct((rows, feature), jnp.bfloat16),
        scratch_shapes=[pltpu.VMEM((rows, feature), jnp.float32)],
        compiler_params=pltpu.CompilerParams(vmem_limit_bytes=VMEM_LIMIT),
        cost_estimate=pl.CostEstimate(
            flops=2 * rows * ff * feature,
            bytes_accessed=2 * ff * feature + 2 * ff * rows,
            transcendentals=0,
        ),
        name="back",
    )(weights, activity)


def window_index(row, col, tile):
    wins = (tile + 2 * margin_cells) // window_side
    window = (row // window_side) * wins + col // window_side
    return (window * window_side + row % window_side) * window_side + col % window_side


def into_windows(tile):
    ext = tile + 2 * margin_cells
    edge, strip = margin_cells * tile, margin_cells * ext
    piece = lax.broadcasted_iota(jnp.int32, (1, ext * ext), 1)
    base = tile * tile
    row, col = margin_cells + piece // tile, margin_cells + piece % tile
    low = piece - base
    row = jnp.where(piece >= base, low // tile, row)
    high = piece - (base + edge)
    row = jnp.where(piece >= base + edge, tile + margin_cells + high // tile, row)
    left = piece - (base + 2 * edge)
    side = piece >= base + 2 * edge
    row = jnp.where(side, left // margin_cells, row)
    col = jnp.where(side, left % margin_cells, col)
    right = left - strip
    side = piece >= base + 2 * edge + strip
    row = jnp.where(side, right // margin_cells, row)
    col = jnp.where(side, tile + margin_cells + right % margin_cells, col)
    place = window_index(row, col, tile)
    return one_hot(lax.broadcasted_iota(jnp.int32, (ext * ext, ext * ext), 0) == place)


def out_of_windows(tile):
    ext = tile + 2 * margin_cells
    token = lax.broadcasted_iota(jnp.int32, (tile * tile, 1), 0)
    place = window_index(token // tile + margin_cells, token % tile + margin_cells, tile)
    return one_hot(lax.broadcasted_iota(jnp.int32, (tile * tile, ext * ext), 1) == place)


def front_kernel(
    at_ref, tok_ref, low_ref, high_ref, left_ref, right_ref, wqkv_ref, wproj_ref, mixed_ref, qkv_ref, ctx_ref
):
    bf16, f32 = jnp.bfloat16, jnp.float32
    tokens = tok_ref[...]
    count, feature = tokens.shape
    cells = window_side * window_side
    head = feature // HEADS
    group = 128 // head
    pieces = jnp.concatenate(
        [tokens, low_ref[...], high_ref[...], left_ref[...], right_ref[...]], axis=0
    )
    placed = nn(into_windows(math.isqrt(count)), pieces).astype(bf16)
    qkv_ref[...] = jnp.dot(placed, wqkv_ref[...], preferred_element_type=f32).astype(bf16)
    first_row, last_row = at_ref[0] == 0, at_ref[0] == at_ref[1] - 1
    first_col, last_col = at_ref[2] == 0, at_ref[2] == at_ref[3] - 1
    lane = lax.broadcasted_iota(jnp.int32, (1, 128), 1)
    own = [
        ((lane >= h * head) & (lane < (h + 1) * head)).astype(f32) for h in range(group)
    ]
    own16 = [o.astype(bf16) for o in own]
    key = lax.broadcasted_iota(jnp.int32, (cells, 128), 0)
    key_row, key_col = key // window_side, key % window_side
    half = window_side // 2
    low_bias = jnp.float32(-1e30)
    edge_bias = {
        (0, 0): jnp.where(key_row < half, jnp.where(first_row, low_bias, 0.0), 0.0),
        (0, 2): jnp.where(key_row >= half, jnp.where(last_row, low_bias, 0.0), 0.0),
        (1, 0): jnp.where(key_col < half, jnp.where(first_col, low_bias, 0.0), 0.0),
        (1, 2): jnp.where(key_col >= half, jnp.where(last_col, low_bias, 0.0), 0.0),
    }
    scale = 1.0 / math.sqrt(head)
    for window in range(9):
        wi, wj = window // 3, window % 3
        bias = None
        if wi != 1:
            bias = edge_bias[0, wi]
        if wj != 1:
            bias = edge_bias[1, wj] if bias is None else bias + edge_bias[1, wj]
        if bias is not None:
            bias = jnp.concatenate([bias] * (group * cells // 128), axis=1)
        rows = slice(window * cells, (window + 1) * cells)
        for g in range(feature // 128):
            q = qkv_ref[rows, g * 128 : (g + 1) * 128]
            k = qkv_ref[rows, feature + g * 128 : feature + (g + 1) * 128]
            v = qkv_ref[rows, 2 * feature + g * 128 : 2 * feature + (g + 1) * 128]
            spread = jnp.concatenate([q * o for o in own16], axis=0)
            scores = nt(k, spread)
            if bias is not None:
                scores = scores + bias
            peak = jnp.max(scores, axis=0, keepdims=True)
            weights = jnp.exp((scores - peak) * scale)
            probs = (weights * (1.0 / jnp.sum(weights, axis=0, keepdims=True))).astype(bf16)
            wide = tn(probs, v)
            mine = wide[:cells] * own[0]
            for h in range(1, group):
                mine = mine + wide[h * cells : (h + 1) * cells] * own[h]
            ctx_ref[rows, g * 128 : (g + 1) * 128] = mine.astype(bf16)
    context = nn(out_of_windows(math.isqrt(count)), ctx_ref[...]).astype(bf16)
    attended = jnp.dot(context, wproj_ref[...], preferred_element_type=f32)
    centred = attended - jnp.mean(attended, axis=-1, keepdims=True)
    spread_of = jnp.mean(centred * centred, axis=-1, keepdims=True)
    mixed = (tokens.astype(f32) + centred * lax.rsqrt(spread_of + 1e-05)).astype(bf16)
    mixed_ref[...] = mixed


def front(at, tokens, low, high, left, right, w_qkv, w_proj):
    count, feature = tokens.shape
    ext = (math.isqrt(count) + 2 * margin_cells) ** 2
    smem = pl.BlockSpec(memory_space=pltpu.SMEM)
    vmem = pl.BlockSpec(memory_space=pltpu.VMEM)
    return vmem_call(
        front_kernel,
        [((count, feature), jnp.bfloat16)],
        "front",
        4_000_000_000,
        in_specs=[smem] + [vmem] * 7,
        scratch_shapes=[
            pltpu.VMEM((ext, 3 * feature), jnp.bfloat16),
            pltpu.VMEM((ext, feature), jnp.bfloat16),
        ],
    )(at, tokens, low, high, left, right, w_qkv, w_proj)[0]


def shifts(axis):
    count = lax.axis_size(axis)
    forward = [(i, i + 1) for i in range(count - 1)]
    return forward, [(target, source) for source, target in forward]


def sharing():
    count, width = lax.axis_size("rep"), lax.axis_size("exp")
    groups = [list(range(parity, count, 2)) for parity in range(2)]
    swap = []
    for rep in range(count):
        for exp in range(width):
            partner = (rep + 1) % count if (rep + exp) % 2 == 0 else (rep - 1) % count
            swap.append((rep * width + exp, partner * width + exp))
    return groups, swap


def per_device(tokens, gate, route, cotangent, w_qkv, w_proj, w_up, w_down):
    tile_rows, tile_cols, feature = tokens.shape
    tok_count = tile_rows * tile_cols
    margin = margin_cells
    experts = lax.axis_size("exp")
    capacity = max(2, 3 * tok_count // (2 * experts))
    slot_count = 2 * experts * capacity
    bf16, f32 = jnp.bfloat16, jnp.float32
    rows_of = ((slot_count, feature), bf16)
    groups, swap = sharing()

    def exchange(rows):
        return lax.ppermute(rows, ("rep", "exp"), swap)

    def dispatch(rows):
        blocks = rows.reshape(experts, -1, feature)
        return lax.all_to_all(blocks, "exp", 0, 0, tiled=True).reshape(-1, feature)

    forward, backward = shifts("rep")
    low = lax.ppermute(tokens[tile_rows - margin :], "rep", forward)
    high = lax.ppermute(tokens[:margin], "rep", backward)
    gate_rows = gate.reshape(tok_count, 1)
    [give] = vmem_call(
        upstream_kernel, [((tok_count + EXTRA, feature), bf16)], "upstream", 1_000_000, count=3
    )(route.reshape(1, tok_count), gate_rows, cotangent.reshape(tok_count, feature))
    got = exchange(give)
    w_up, w_down, give = lax.optimization_barrier((w_up, w_down, give))
    weights = lax.all_gather(
        jnp.concatenate([w_up, w_down], axis=0),
        "rep",
        axis=0,
        tiled=False,
        axis_index_groups=groups,
    )
    forward, backward = shifts("exp")

    def strip(cols):
        parts = [low[:, cols], tokens[:, cols], high[:, cols]]
        return jnp.concatenate(parts, axis=0).reshape(-1, feature)

    left = lax.ppermute(strip(slice(tile_cols - margin, tile_cols)), "exp", forward)
    right = lax.ppermute(strip(slice(0, margin)), "exp", backward)
    at = jnp.stack(
        [
            lax.axis_index("rep"),
            jnp.int32(lax.axis_size("rep")),
            lax.axis_index("exp"),
            jnp.int32(experts),
        ]
    ).astype(jnp.int32)
    mixed = front(
        at,
        tokens.reshape(tok_count, feature),
        low.reshape(-1, feature),
        high.reshape(-1, feature),
        left,
        right,
        w_qkv,
        w_proj,
    )
    got_mixed = exchange(mixed)
    got, mixed = lax.optimization_barrier((got, mixed))
    slots_g, target = vmem_call(
        functools.partial(grad_slots_kernel, experts, capacity),
        [rows_of, ((2, tok_count), jnp.int32)],
        "grad_slots",
        500_000_000,
        count=2,
    )(give, got)
    slot_g = dispatch(slots_g)
    [slots_x] = vmem_call(token_slots_kernel, [rows_of], "token_slots", 400_000_000, count=3)(
        target, mixed, got_mixed
    )
    slot_x = dispatch(slots_x)
    grads, hidden, pre_grad = middle(weights, slot_x, slot_g)
    summed = lax.psum_scatter(
        grads, "rep", scatter_dimension=0, tiled=True, axis_index_groups=groups
    )

    def exchanged(rows):
        [theirs] = vmem_call(
            back_rows_kernel, [((tok_count, feature), bf16)], "back_rows", 200_000_000, count=2
        )(target, rows)
        return exchange(theirs)

    back_out = dispatch(back(weights, hidden, 1))
    back_in = dispatch(back(weights, pre_grad, 0))
    got_out = exchanged(back_out)
    back_in, got_out = lax.optimization_barrier((back_in, got_out))
    layer_out, input_grad = vmem_call(
        combine_kernel, [((tok_count, feature), bf16)] * 2, "combine", 400_000_000, count=7
    )(target, back_out, got_out, back_in, exchanged(back_in), mixed, gate_rows)
    grad_up, grad_down = vmem_call(
        functools.partial(gradients_kernel, 1.0 / lax.axis_size("rep")),
        [(w_up.shape, f32)] * 2,
        "gradients",
        1_000_000,
        count=1,
    )(summed)
    return (
        layer_out.reshape(tile_rows, tile_cols, feature),
        input_grad.reshape(tile_rows, tile_cols, feature),
        grad_up,
        grad_down,
    )


def solution(mesh):
    placed = (
        P("rep", "exp", None),
        P("rep", "exp"),
        P("rep", "exp", None, None),
        P("rep", "exp", None),
        P(),
        P(),
        P("exp", "rep", None),
        P("exp", "rep", None),
    )
    return jax.shard_map(
        per_device,
        mesh=mesh,
        in_specs=placed,
        out_specs=(
            P("rep", "exp", None),
            P("rep", "exp", None),
            P("exp", "rep", None),
            P("exp", "rep", None),
        ),
        check_vma=False,
    )
```
